512 devices in a mesh: rows: 128 (over z, y, core), grp: 4 (over x).
Axes of the slice: x: 4, y: 8, z: 8, core: 2. Of those that a mesh axis runs over, the one named last changes fastest.
Arguments:
- embeddings: float32 [65536, 768], P(('rows', 'grp')), may hold values from -100 to 100
- assignments: int32 [65536], P(('rows', 'grp')), may hold values from 0 to 16383, as said below
Outputs:
- whitened: float32 [65536, 768], P(('rows', 'grp'))
- centroid_means: float32 [16384, 768], P(('rows', 'grp'))
The draws below stay inside these ranges and needn't reach their ends.
Inputs may be any that keep to these rules, and one draw needn't show every extreme that they name: `assignments`: owner o holds the 128 centroids o * 128 to (o + 1) * 128 - 1. The 128 rows of one device name centroids of at most 2 rows for any one owner, and exactly 2 for some owner. Some centroids are named by no row.
All inputs are finite; a program needn't handle non-finite values.
Results may differ from the reference program's by a relative error of at most 0.00007.
Values sent between devices are 32-bit elements; how exact they have to be, the bound alone decides.
No kernel may reach another device: no remote copies, remote signals or barrier semaphores. Data moves between devices by JAX's collectives and lax.ppermute only.
A program may use at most 64 MiB of HBM per device.

```python
import math
import jax
import jax.numpy as jnp
from jax import lax

D = 768
CENTROIDS = 16384
R_DEV = 128
CAP = 2
TOTAL_ROWS = 65536
N_ROWS = 128


def draw_embeddings(key, part):
    first, second = jax.random.split(jax.random.fold_in(key, 11), 2)
    blocks = TOTAL_ROWS // R_DEV
    block_index = jnp.arange(TOTAL_ROWS, dtype=jnp.int32) // R_DEV
    device_scale = 3.0 ** (0.5 * block_index.astype(jnp.float32) / max(blocks - 1, 1))
    base = jnp.clip(jax.random.normal(first, (TOTAL_ROWS, D), jnp.float32), -5.0, 5.0)
    row_scale = jnp.exp(jax.random.uniform(second, (TOTAL_ROWS,), jnp.float32, 0.0, math.log(10.0)))
    values = base * row_scale[:, None]
    return values * device_scale[:, None]


def draw_assignments(key, part):
    per_owner = CENTROIDS // N_ROWS
    blocks = TOTAL_ROWS // R_DEV
    offsets = jax.random.randint(jax.random.fold_in(key, 7), (N_ROWS,), 0, per_owner)
    block_keys = jax.random.split(jax.random.fold_in(key, 5), blocks)

    def one_block(block_key):
        kfirst, ksecond, kthird, kfourth = jax.random.split(block_key, 4)
        chosen = jax.random.randint(kfirst, (), 0, N_ROWS)
        others = jnp.tile(jnp.arange(1, N_ROWS, dtype=jnp.int32), CAP)
        others = jax.random.permutation(ksecond, others)[:R_DEV - CAP]
        owners = jnp.concatenate([jnp.zeros((CAP,), jnp.int32), others])
        owners = (owners + chosen) % N_ROWS
        owners = jax.random.permutation(kthird, owners)
        tries = jax.random.randint(kfourth, (3, R_DEV), 0, per_owner)
        local = (jnp.min(tries, axis=0) + offsets[owners]) % per_owner
        return owners * per_owner + local
    return jax.vmap(one_block)(block_keys).reshape(TOTAL_ROWS).astype(jnp.int32)


def setup_inputs(seed: int = 0) -> dict:
    streams_of = jax.random.split(jax.random.key(seed), 3)
    return {
        "embeddings": draw_embeddings(jax.random.fold_in(streams_of[2], 71), 0),
        "assignments": draw_assignments(jax.random.fold_in(streams_of[2], 71), 0),
    }


def reference(embeddings, assignments):
    total = embeddings.shape[0]
    width = embeddings.shape[1]
    gram = jnp.dot(embeddings.T.astype(jnp.float32), embeddings.astype(jnp.float32), precision=lax.Precision.HIGHEST, preferred_element_type=jnp.float32)
    gram = gram / total + 1e-05 * jnp.eye(width, dtype=jnp.float32)
    factor = jnp.linalg.cholesky(gram)
    whitened = lax.linalg.triangular_solve(factor, embeddings, left_side=False, lower=True, transpose_a=True)
    list_sums = jax.ops.segment_sum(whitened, assignments, num_segments=CENTROIDS)
    ones = jnp.ones(assignments.shape, dtype=jnp.float32)
    list_counts = jax.ops.segment_sum(ones, assignments, num_segments=CENTROIDS)
    centroid_means = list_sums / jnp.maximum(list_counts, 1.0)[:, None]
    return (whitened, centroid_means)
```

```python
import jax
import jax.numpy as jnp
from jax import lax
from jax.sharding import Mesh, PartitionSpec as P

CENTROIDS = 16384
CAP = 2
B = 128


def spread(value, axis):
    peers = lax.axis_size(axis)
    copies = jnp.broadcast_to(value[None], (peers, *value.shape))
    return lax.all_to_all(copies, axis, 0, 0, tiled=True)


def reduced(pieces, axis):
    return jnp.sum(lax.all_to_all(pieces, axis, 0, 0, tiled=True), axis=0)


def gram_sum(part):
    mine = reduced(part.reshape(8, 336, B), ("core", "x"))
    mine = reduced(mine.reshape(8, 42, B), "y")
    mine = jnp.sum(spread(mine, "z"), axis=0)
    mine = spread(mine, "y").reshape(336, B)
    return spread(mine, ("core", "x")).reshape(2688, B)


def body(embeddings, assignments):
    rows_here, width = embeddings.shape
    rows_axes = ("z", "y", "core")
    owners = lax.axis_size(rows_axes)
    total = rows_here * owners * lax.axis_size("x")
    per_owner = CENTROIDS // owners
    n = width // B
    part = jnp.dot(
        embeddings.T, embeddings, precision=lax.Precision.HIGHEST, preferred_element_type=jnp.float32
    )
    lower = [(i, j) for j in range(n) for i in range(j, n)]
    part = jnp.concatenate([part[i * B : i * B + B, j * B : j * B + B] for i, j in lower], axis=0)

    target = assignments // per_owner
    local = assignments % per_owner
    same = target[:, None] == target[None, :]
    before = jnp.arange(rows_here)[:, None] > jnp.arange(rows_here)[None, :]
    rank = jnp.sum((same & before).astype(jnp.int32), axis=1)
    slot = target * CAP + rank
    chosen = slot[None, :] == jnp.arange(owners * CAP, dtype=jnp.int32)[:, None]
    outgoing = jnp.dot(
        chosen.astype(jnp.float32), embeddings, precision=lax.Precision.HIGHEST, preferred_element_type=jnp.float32
    )
    labels = jnp.sum(jnp.where(chosen, (local + 1)[None, :], 0), axis=1) - 1
    outgoing = outgoing.reshape(owners, CAP * width)
    labels = jnp.pad(labels.reshape(owners, CAP).astype(jnp.float32), ((0, 0), (0, B - CAP)))
    packed = jnp.concatenate([outgoing, labels], axis=1).reshape(owners, CAP * n + 1, B)
    packed = lax.all_to_all(packed, rows_axes, 0, 0, tiled=True).reshape(owners, CAP * width + B)
    incoming = packed[:, : CAP * width].reshape(owners * CAP, width)
    tags = packed[:, CAP * width : CAP * width + CAP].reshape(-1).astype(jnp.int32)
    member = (tags[None, :] == jnp.arange(per_owner, dtype=jnp.int32)[:, None]).astype(jnp.float32)
    sums = jnp.dot(member, incoming, precision=lax.Precision.HIGHEST, preferred_element_type=jnp.float32)
    counts = jnp.sum(member, axis=1)
    groups = lax.axis_size("x")
    keep = per_owner // groups
    sums = sums.reshape(groups, keep * n, B)
    counts = jnp.pad(counts.reshape(groups, 1, keep), ((0, 0), (0, 7), (0, B - keep)))
    mine = reduced(jnp.concatenate([sums, counts], axis=1), "x")
    sums = mine[: keep * n].reshape(keep, width)
    counts = mine[keep * n, :keep]

    whole = gram_sum(part)
    at = {ij: whole[k * B : k * B + B] for k, ij in enumerate(lower)}
    grid = [[at[i, j] if i >= j else at[j, i].T for j in range(n)] for i in range(n)]
    gram = jnp.block(grid) / total + 1e-05 * jnp.eye(width, dtype=jnp.float32)
    factor = lax.linalg.cholesky(gram, symmetrize_input=False)
    means = sums / jnp.maximum(counts, 1.0)[:, None]
    solved = lax.linalg.triangular_solve(
        factor, jnp.concatenate([embeddings, means], axis=0), left_side=False, lower=True, transpose_a=True
    )
    return solved[:rows_here], solved[rows_here:]


def solution(mesh):
    fine = Mesh(mesh.devices.reshape(8, 8, 2, 4), ("z", "y", "core", "x"))
    spec = ("z", "y", "core", "x")
    return jax.shard_map(
        body,
        mesh=fine,
        in_specs=(P(spec, None), P(spec)),
        out_specs=(P(spec, None), P(spec, None)),
        check_vma=False,
    )
```

```python
import functools

import jax
import jax.numpy as jnp
from jax import lax
from jax.experimental import pallas as pl
from jax.experimental.pallas import tpu as pltpu
from jax.sharding import Mesh, PartitionSpec as P

CENTROIDS = 16384
CAP = 2
B = 128

HI = lax.Precision.HIGHEST
NT = (((1,), (1,)), ((), ()))


def mul_t(a, b):
    return lax.dot_general(a, b, NT, precision=HI, preferred_element_type=jnp.float32)


def inverse_factor(block):
    groups = B // 8
    tiles = [block[8 * i : 8 * i + 8] for i in range(groups)]
    lane = lax.broadcasted_iota(jnp.int32, (8, B), 1)
    sub = lax.broadcasted_iota(jnp.int32, (8, B), 0)
    for g in range(groups):
        done = (lane >= 8 * g) & (lane < 8 * g + 8)
        cols = [[jnp.broadcast_to(t[:, 8 * g + k : 8 * g + k + 1], (8, B)) for k in range(8)] for t in tiles[g:]]
        here = jnp.where(lane == sub + 8 * g, 1.0, jnp.where(done, 0.0, tiles[g]))
        rows = [here[k : k + 1] for k in range(8)]
        small = [[cols[0][p][k : k + 1] for p in range(8)] for k in range(8)]
        scaled = []
        for p in range(8):
            r = 1.0 / small[p][p]
            for k in range(p + 1, 8):
                m = small[k][p] * r
                for q in range(k, 8):
                    small[q][k] = small[q][k] - m * small[q][p]
                rows[k] = rows[k] - m * rows[p]
                for c in cols[1:]:
                    c[k] = c[k] - m * c[p]
            scaled.append(rows[p] * r)
        for i in range(g + 1, groups):
            new = jnp.where(done, 0.0, tiles[i])
            for p in range(8):
                new = new - cols[i - g][p] * scaled[p]
            tiles[i] = new
        tiles[g] = jnp.concatenate([rows[k] * lax.rsqrt(small[k][k]) for k in range(8)], axis=0)
    row = lax.broadcasted_iota(jnp.int32, (B, B), 0)
    col = lax.broadcasted_iota(jnp.int32, (B, B), 1)
    return jnp.where(col <= row, jnp.concatenate(tiles, axis=0), 0.0)


def first(j, n):
    return (j * n - j * (j - 1) // 2) * B


def whiten_kernel(total, n, gram_ref, x_ref, out_ref, a_ref, x_blocks, inv_ref):
    row = lax.broadcasted_iota(jnp.int32, (B, B), 0)
    col = lax.broadcasted_iota(jnp.int32, (B, B), 1)
    a_ref[...] = gram_ref[...] * (1.0 / total)
    for j in range(n):
        at = first(j, n)
        a_ref[at : at + B] += jnp.where(row == col, 1e-05, 0.0)
        x_blocks[j] = x_ref[:, j * B : j * B + B]

    def step(k, carry):
        inv_ref[...] = inverse_factor(a_ref[pl.ds(pl.multiple_of(first(k, n), B), B)])
        for now in range(n):

            @pl.when(k == now)
            def _():
                inv = inv_ref[...]
                at = first(now, n) + B
                below = (n - now - 1) * B
                solved = mul_t(x_blocks[now], inv)
                out_ref[:, now * B : now * B + B] = solved
                if below:
                    panel = mul_t(a_ref[at : at + below], inv)
                    for j in range(now + 1, n):
                        top = (j - now - 1) * B
                        to = first(j, n)
                        part = panel[top : top + B]
                        a_ref[to : to + (n - j) * B] -= mul_t(panel[top:], part)
                        x_blocks[j] -= mul_t(solved, part)

        return carry

    lax.fori_loop(0, n, step, 0)


def whiten(gram, x, total):
    n = x.shape[1] // B
    return pl.pallas_call(
        functools.partial(whiten_kernel, total, n),
        out_shape=jax.ShapeDtypeStruct(x.shape, jnp.float32),
        in_specs=[pl.BlockSpec(memory_space=pltpu.VMEM)] * 2,
        out_specs=pl.BlockSpec(memory_space=pltpu.VMEM),
        scratch_shapes=[
            pltpu.VMEM(gram.shape, jnp.float32),
            pltpu.VMEM((n, x.shape[0], B), jnp.float32),
            pltpu.VMEM((B, B), jnp.float32),
        ],
        compiler_params=pltpu.CompilerParams(vmem_limit_bytes=32 << 20),
        cost_estimate=pl.CostEstimate(flops=20_000_000_000, bytes_accessed=4_000_000, transcendentals=0),
        name="whiten",
    )(gram, x)


def spread(value, axis):
    peers = lax.axis_size(axis)
    copies = jnp.broadcast_to(value[None], (peers, *value.shape))
    return lax.all_to_all(copies, axis, 0, 0, tiled=True)


def reduced(pieces, axis):
    return jnp.sum(lax.all_to_all(pieces, axis, 0, 0, tiled=True), axis=0)


def gram_sum(part):
    mine = reduced(part.reshape(8, 336, B), ("core", "x"))
    mine = reduced(mine.reshape(8, 42, B), "y")
    mine = jnp.sum(spread(mine, "z"), axis=0)
    mine = spread(mine, "y").reshape(336, B)
    return spread(mine, ("core", "x")).reshape(2688, B)


def body(embeddings, assignments):
    rows_here, width = embeddings.shape
    rows_axes = ("z", "y", "core")
    owners = lax.axis_size(rows_axes)
    total = rows_here * owners * lax.axis_size("x")
    per_owner = CENTROIDS // owners
    n = width // B
    part = jnp.dot(
        embeddings.T, embeddings, precision=lax.Precision.HIGHEST, preferred_element_type=jnp.float32
    )
    lower = [(i, j) for j in range(n) for i in range(j, n)]
    part = jnp.concatenate([part[i * B : i * B + B, j * B : j * B + B] for i, j in lower], axis=0)

    target = assignments // per_owner
    local = assignments % per_owner
    same = target[:, None] == target[None, :]
    before = jnp.arange(rows_here)[:, None] > jnp.arange(rows_here)[None, :]
    rank = jnp.sum((same & before).astype(jnp.int32), axis=1)
    slot = target * CAP + rank
    chosen = slot[None, :] == jnp.arange(owners * CAP, dtype=jnp.int32)[:, None]
    outgoing = jnp.dot(
        chosen.astype(jnp.float32), embeddings, precision=lax.Precision.HIGHEST, preferred_element_type=jnp.float32
    )
    labels = jnp.sum(jnp.where(chosen, (local + 1)[None, :], 0), axis=1) - 1
    outgoing = outgoing.reshape(owners, CAP * width)
    labels = jnp.pad(labels.reshape(owners, CAP).astype(jnp.float32), ((0, 0), (0, B - CAP)))
    packed = jnp.concatenate([outgoing, labels], axis=1).reshape(owners, CAP * n + 1, B)
    packed = lax.all_to_all(packed, rows_axes, 0, 0, tiled=True).reshape(owners, CAP * width + B)
    incoming = packed[:, : CAP * width].reshape(owners * CAP, width)
    tags = packed[:, CAP * width : CAP * width + CAP].reshape(-1).astype(jnp.int32)
    member = (tags[None, :] == jnp.arange(per_owner, dtype=jnp.int32)[:, None]).astype(jnp.float32)
    sums = jnp.dot(member, incoming, precision=lax.Precision.HIGHEST, preferred_element_type=jnp.float32)
    counts = jnp.sum(member, axis=1)
    groups = lax.axis_size("x")
    keep = per_owner // groups
    sums = sums.reshape(groups, keep * n, B)
    counts = jnp.pad(counts.reshape(groups, 1, keep), ((0, 0), (0, 7), (0, B - keep)))
    mine = reduced(jnp.concatenate([sums, counts], axis=1), "x")
    sums = mine[: keep * n].reshape(keep, width)
    counts = mine[keep * n, :keep]

    whole = gram_sum(part)
    means = sums / jnp.maximum(counts, 1.0)[:, None]
    solved = whiten(whole, jnp.concatenate([embeddings, means], axis=0), total)
    return solved[:rows_here], solved[rows_here:]


def solution(mesh):
    fine = Mesh(mesh.devices.reshape(8, 8, 2, 4), ("z", "y", "core", "x"))
    spec = ("z", "y", "core", "x")
    return jax.shard_map(
        body,
        mesh=fine,
        in_specs=(P(spec, None), P(spec)),
        out_specs=(P(spec, None), P(spec, None)),
        check_vma=False,
    )
```

```python
import functools

import jax
import jax.numpy as jnp
from jax import lax
from jax.experimental import pallas as pl
from jax.experimental.pallas import tpu as pltpu
from jax.sharding import Mesh, PartitionSpec as P

CENTROIDS = 16384
CAP = 2
B = 128

VMEM = pl.BlockSpec(memory_space=pltpu.VMEM)
SCALAR = pl.BlockSpec(memory_space=pltpu.SMEM)
HI = lax.Precision.HIGHEST
NT = (((1,), (1,)), ((), ()))


def mul_t(a, b):
    return lax.dot_general(a, b, NT, precision=HI, preferred_element_type=jnp.float32)


def inverse_factor(block):
    groups = B // 8
    tiles = [block[8 * i : 8 * i + 8] for i in range(groups)]
    lane = lax.broadcasted_iota(jnp.int32, (8, B), 1)
    sub = lax.broadcasted_iota(jnp.int32, (8, B), 0)
    for g in range(groups):
        done = (lane >= 8 * g) & (lane < 8 * g + 8)
        cols = [[jnp.broadcast_to(t[:, 8 * g + k : 8 * g + k + 1], (8, B)) for k in range(8)] for t in tiles[g:]]
        here = jnp.where(lane == sub + 8 * g, 1.0, jnp.where(done, 0.0, tiles[g]))
        rows = [here[k : k + 1] for k in range(8)]
        small = [[cols[0][p][k : k + 1] for p in range(8)] for k in range(8)]
        scaled = []
        for p in range(8):
            r = 1.0 / small[p][p]
            for k in range(p + 1, 8):
                m = small[k][p] * r
                for q in range(k, 8):
                    small[q][k] = small[q][k] - m * small[q][p]
                rows[k] = rows[k] - m * rows[p]
                for c in cols[1:]:
                    c[k] = c[k] - m * c[p]
            scaled.append(rows[p] * r)
        for i in range(g + 1, groups):
            new = jnp.where(done, 0.0, tiles[i])
            for p in range(8):
                new = new - cols[i - g][p] * scaled[p]
            tiles[i] = new
        tiles[g] = jnp.concatenate([rows[k] * lax.rsqrt(small[k][k]) for k in range(8)], axis=0)
    row = lax.broadcasted_iota(jnp.int32, (B, B), 0)
    col = lax.broadcasted_iota(jnp.int32, (B, B), 1)
    return jnp.where(col <= row, jnp.concatenate(tiles, axis=0), 0.0)


def first(j, n):
    return (j * n - j * (j - 1) // 2) * B


def whiten_kernel(total, n, bit_ref, mine_ref, other_ref, x_ref, out_ref, a_ref, x_blocks, inv_ref):
    row = lax.broadcasted_iota(jnp.int32, (B, B), 0)
    col = lax.broadcasted_iota(jnp.int32, (B, B), 1)
    half = mine_ref.shape[0]
    bit = bit_ref[0]
    a_ref[pl.ds(pl.multiple_of(bit * half, 8), half)] = mine_ref[...] * (1.0 / total)
    a_ref[pl.ds(pl.multiple_of((1 - bit) * half, 8), half)] = other_ref[...] * (1.0 / total)
    for j in range(n):
        at = first(j, n)
        a_ref[at : at + B] += jnp.where(row == col, 1e-05, 0.0)
        x_blocks[j] = x_ref[:, j * B : j * B + B]

    def step(k, carry):
        inv_ref[...] = inverse_factor(a_ref[pl.ds(pl.multiple_of(first(k, n), B), B)])
        for now in range(n):

            @pl.when(k == now)
            def _():
                inv = inv_ref[...]
                at = first(now, n) + B
                below = (n - now - 1) * B
                solved = mul_t(x_blocks[now], inv)
                out_ref[:, now * B : now * B + B] = solved
                if below:
                    panel = mul_t(a_ref[at : at + below], inv)
                    for j in range(now + 1, n):
                        top = (j - now - 1) * B
                        to = first(j, n)
                        part = panel[top : top + B]
                        a_ref[to : to + (n - j) * B] -= mul_t(panel[top:], part)
                        x_blocks[j] -= mul_t(solved, part)

        return carry

    lax.fori_loop(0, n, step, 0)


def whiten(bit, mine, other, x, total):
    n = x.shape[1] // B
    return pl.pallas_call(
        functools.partial(whiten_kernel, total, n),
        out_shape=jax.ShapeDtypeStruct(x.shape, jnp.float32),
        in_specs=[SCALAR, VMEM, VMEM, VMEM],
        out_specs=VMEM,
        scratch_shapes=[
            pltpu.VMEM((2 * mine.shape[0], B), jnp.float32),
            pltpu.VMEM((n, x.shape[0], B), jnp.float32),
            pltpu.VMEM((B, B), jnp.float32),
        ],
        compiler_params=pltpu.CompilerParams(vmem_limit_bytes=12 << 20),
        cost_estimate=pl.CostEstimate(flops=20_000_000_000, bytes_accessed=4_000_000, transcendentals=0),
        name="whiten",
    )(bit, mine, other, x)


def gram_kernel(n, bit_ref, x_ref, keep_ref, send_ref, all_ref):
    turned = x_ref[...].T
    for j in range(n):
        all_ref[first(j, n) : first(j + 1, n)] = jnp.dot(
            turned[j * B :], x_ref[:, j * B : j * B + B], precision=HI, preferred_element_type=jnp.float32
        )
    half = keep_ref.shape[0]
    bit = bit_ref[0]
    keep_ref[...] = all_ref[pl.ds(pl.multiple_of(bit * half, 8), half)]
    send_ref[...] = all_ref[pl.ds(pl.multiple_of((1 - bit) * half, 8), half)]


def gram_halves(bit, x):
    n = x.shape[1] // B
    rows = first(n, n)
    return pl.pallas_call(
        functools.partial(gram_kernel, n),
        out_shape=[jax.ShapeDtypeStruct((rows // 2, B), jnp.float32)] * 2,
        in_specs=[SCALAR, VMEM],
        out_specs=[VMEM, VMEM],
        scratch_shapes=[pltpu.VMEM((rows, B), jnp.float32)],
        compiler_params=pltpu.CompilerParams(vmem_limit_bytes=12 << 20),
        cost_estimate=pl.CostEstimate(flops=700_000_000, bytes_accessed=2_000_000, transcendentals=0),
        name="gram",
    )(bit, x)


def cut_kernel(terms, order, at_ref, *refs):
    ins, outs, total_ref = refs[:terms], refs[terms:-1], refs[-1]
    rows = ins[0].shape[0]
    total_ref[:rows] = functools.reduce(lambda a, b: a + b, [r[...] for r in ins])
    if rows < total_ref.shape[0]:
        total_ref[rows:] = jnp.zeros((total_ref.shape[0] - rows, B), jnp.float32)
    size = outs[0].shape[0]
    for s, out in enumerate(outs):
        out[...] = total_ref[pl.ds(pl.multiple_of(order(at_ref[0], s) * size, 8), size)]


def cut(at, arrays, pieces, rows, name):
    return pl.pallas_call(
        functools.partial(cut_kernel, len(arrays), lambda a, s: (a + s) & (pieces - 1)),
        out_shape=[jax.ShapeDtypeStruct((rows // pieces, B), jnp.float32)] * pieces,
        in_specs=[SCALAR] + [VMEM] * len(arrays),
        out_specs=[VMEM] * pieces,
        scratch_shapes=[pltpu.VMEM((rows, B), jnp.float32)],
        compiler_params=pltpu.CompilerParams(vmem_limit_bytes=6 << 20),
        cost_estimate=pl.CostEstimate(flops=1_000_000, bytes_accessed=3_000_000, transcendentals=0),
        name=name,
    )(at, *arrays)


def place_kernel(at_ref, *refs):
    out = refs[-1]
    count = len(refs) - 1
    size = refs[0].shape[0]
    for s in range(count):
        out[pl.ds(pl.multiple_of(((at_ref[0] - s) & (count - 1)) * size, 8), size)] = refs[s][...]


def place(at, arrays, name):
    rows = arrays[0].shape[0] * len(arrays)
    return pl.pallas_call(
        place_kernel,
        out_shape=jax.ShapeDtypeStruct((rows, B), jnp.float32),
        in_specs=[SCALAR] + [VMEM] * len(arrays),
        out_specs=VMEM,
        compiler_params=pltpu.CompilerParams(vmem_limit_bytes=6 << 20),
        cost_estimate=pl.CostEstimate(flops=0, bytes_accessed=1_500_000, transcendentals=0),
        name=name,
    )(at, *arrays)


def shifted(value, axis, by):
    size = lax.axis_size(axis)
    return lax.ppermute(value, axis, [(i, (i + by) % size) for i in range(size)])


def swapped(value, axis, by):
    return lax.ppermute(value, axis, [(i, i ^ by) for i in range(lax.axis_size(axis))])


def index(axis):
    return lax.axis_index(axis).reshape(1)


def gram_sum(keep, send):
    keep_rows = keep.shape[0]
    x, y = index("x"), index("y")
    pieces = cut(x, [keep, swapped(send, "core", 1)], 4, keep_rows, "cut_x")
    terms = [pieces[0]] + [shifted(pieces[s], "x", s) for s in (1, 2, 3)]
    rows = 384
    for by in (1, 2, 4):
        keep, send = cut((y // by) % 2, terms, 2, rows, "cut_y")
        terms = [keep, swapped(send, "y", by)]
        rows //= 2
    mine = terms[0] + terms[1]
    for by in (1, 2, 4):
        mine = mine + swapped(mine, "z", by)
    for by in (4, 2, 1):
        other = swapped(mine, "y", by)
        mine = place((y // by) % 2, [mine, other], "place_y")
    mine = mine[: keep_rows // 4]
    mine = place(x, [mine] + [shifted(mine, "x", s) for s in (1, 2, 3)], "place_x")
    return mine, swapped(mine, "core", 1)


def reduced(pieces, axis):
    return jnp.sum(lax.all_to_all(pieces, axis, 0, 0, tiled=True), axis=0)


def body(embeddings, assignments):
    rows_here, width = embeddings.shape
    rows_axes = ("z", "y", "core")
    owners = lax.axis_size(rows_axes)
    total = rows_here * owners * lax.axis_size("x")
    per_owner = CENTROIDS // owners
    n = width // B
    bit = index("core")
    half, send = gram_halves(bit, embeddings)

    target = assignments // per_owner
    local = assignments % per_owner
    same = target[:, None] == target[None, :]
    before = jnp.arange(rows_here)[:, None] > jnp.arange(rows_here)[None, :]
    rank = jnp.sum((same & before).astype(jnp.int32), axis=1)
    slot = target * CAP + rank
    chosen = slot[None, :] == jnp.arange(owners * CAP, dtype=jnp.int32)[:, None]
    outgoing = jnp.dot(
        chosen.astype(jnp.float32), embeddings, precision=lax.Precision.HIGHEST, preferred_element_type=jnp.float32
    )
    labels = jnp.sum(jnp.where(chosen, (local + 1)[None, :], 0), axis=1) - 1
    outgoing = outgoing.reshape(owners, CAP * width)
    labels = jnp.pad(labels.reshape(owners, CAP).astype(jnp.float32), ((0, 0), (0, B - CAP)))
    packed = jnp.concatenate([outgoing, labels], axis=1).reshape(owners, CAP * n + 1, B)
    packed = lax.all_to_all(packed, rows_axes, 0, 0, tiled=True).reshape(owners, CAP * width + B)
    incoming = packed[:, : CAP * width].reshape(owners * CAP, width)
    tags = packed[:, CAP * width : CAP * width + CAP].reshape(-1).astype(jnp.int32)
    member = (tags[None, :] == jnp.arange(per_owner, dtype=jnp.int32)[:, None]).astype(jnp.float32)
    sums = jnp.dot(member, incoming, precision=lax.Precision.HIGHEST, preferred_element_type=jnp.float32)
    counts = jnp.sum(member, axis=1)
    groups = lax.axis_size("x")
    keep = per_owner // groups
    sums = sums.reshape(groups, keep * n, B)
    counts = jnp.pad(counts.reshape(groups, 1, keep), ((0, 0), (0, 7), (0, B - keep)))
    mine = reduced(jnp.concatenate([sums, counts], axis=1), "x")
    sums = mine[: keep * n].reshape(keep, width)
    counts = mine[keep * n, :keep]

    mine, other = gram_sum(half, send)
    means = sums / jnp.maximum(counts, 1.0)[:, None]
    solved = whiten(bit, mine, other, jnp.concatenate([embeddings, means], axis=0), total)
    return solved[:rows_here], solved[rows_here:]


def solution(mesh):
    fine = Mesh(mesh.devices.reshape(8, 8, 2, 4), ("z", "y", "core", "x"))
    spec = ("z", "y", "core", "x")
    return jax.shard_map(
        body,
        mesh=fine,
        in_specs=(P(spec, None), P(spec)),
        out_specs=(P(spec, None), P(spec, None)),
        check_vma=False,
    )
```

```python
import functools

import jax
import jax.numpy as jnp
from jax import lax
from jax.experimental import pallas as pl
from jax.experimental.pallas import tpu as pltpu
from jax.sharding import Mesh, PartitionSpec as P

CENTROIDS = 16384
CAP = 2
B = 128

VMEM = pl.BlockSpec(memory_space=pltpu.VMEM)
SCALAR = pl.BlockSpec(memory_space=pltpu.SMEM)
HI = lax.Precision.HIGHEST
NT = (((1,), (1,)), ((), ()))


def mul_t(a, b):
    return lax.dot_general(a, b, NT, precision=HI, preferred_element_type=jnp.float32)


def inverse_factor(block):
    groups = B // 8
    tiles = [block[8 * i : 8 * i + 8] for i in range(groups)]
    lane = lax.broadcasted_iota(jnp.int32, (8, B), 1)
    sub = lax.broadcasted_iota(jnp.int32, (8, B), 0)
    for g in range(groups):
        done = (lane >= 8 * g) & (lane < 8 * g + 8)
        cols = [[jnp.broadcast_to(t[:, 8 * g + k : 8 * g + k + 1], (8, B)) for k in range(8)] for t in tiles[g:]]
        here = jnp.where(lane == sub + 8 * g, 1.0, jnp.where(done, 0.0, tiles[g]))
        rows = [here[k : k + 1] for k in range(8)]
        small = [[cols[0][p][k : k + 1] for p in range(8)] for k in range(8)]
        scaled = []
        for p in range(8):
            r = 1.0 / small[p][p]
            for k in range(p + 1, 8):
                m = small[k][p] * r
                for q in range(k, 8):
                    small[q][k] = small[q][k] - m * small[q][p]
                rows[k] = rows[k] - m * rows[p]
                for c in cols[1:]:
                    c[k] = c[k] - m * c[p]
            scaled.append(rows[p] * r)
        for i in range(g + 1, groups):
            new = jnp.where(done, 0.0, tiles[i])
            for p in range(8):
                new = new - cols[i - g][p] * scaled[p]
            tiles[i] = new
        tiles[g] = jnp.concatenate([rows[k] * lax.rsqrt(small[k][k]) for k in range(8)], axis=0)
    row = lax.broadcasted_iota(jnp.int32, (B, B), 0)
    col = lax.broadcasted_iota(jnp.int32, (B, B), 1)
    return jnp.where(col <= row, jnp.concatenate(tiles, axis=0), 0.0)


def first(j, n):
    return (j * n - j * (j - 1) // 2) * B


def whiten_kernel(total, n, bit_ref, mine_ref, other_ref, x_ref, out_ref, a_ref, x_blocks):
    row = lax.broadcasted_iota(jnp.int32, (B, B), 0)
    col = lax.broadcasted_iota(jnp.int32, (B, B), 1)
    half = mine_ref.shape[0]
    bit = bit_ref[0]
    a_ref[pl.ds(pl.multiple_of(bit * half, 8), half)] = mine_ref[...] * (1.0 / total)
    a_ref[pl.ds(pl.multiple_of((1 - bit) * half, 8), half)] = other_ref[...] * (1.0 / total)
    for j in range(n):
        at = first(j, n)
        a_ref[at : at + B] += jnp.where(row == col, 1e-05, 0.0)
        x_blocks[j] = x_ref[:, j * B : j * B + B]

    inv = inverse_factor(a_ref[:B])
    for now in range(n):
        at = first(now, n) + B
        rest = range(now + 1, n)
        panel = {i: mul_t(a_ref[at + (i - now - 1) * B : at + (i - now) * B], inv) for i in rest}
        if now + 1 < n:
            to = first(now + 1, n)
            following = inverse_factor(a_ref[to : to + B] - mul_t(panel[now + 1], panel[now + 1]))
        solved = mul_t(x_blocks[now], inv)
        out_ref[:, now * B : now * B + B] = solved
        for j in rest:
            for i in range(j, n):
                if i > now + 1:
                    to = first(j, n) + (i - j) * B
                    a_ref[to : to + B] -= mul_t(panel[i], panel[j])
            x_blocks[j] -= mul_t(solved, panel[j])
        if now + 1 < n:
            inv = following


def whiten(bit, mine, other, x, total):
    n = x.shape[1] // B
    return pl.pallas_call(
        functools.partial(whiten_kernel, total, n),
        out_shape=jax.ShapeDtypeStruct(x.shape, jnp.float32),
        in_specs=[SCALAR, VMEM, VMEM, VMEM],
        out_specs=VMEM,
        scratch_shapes=[
            pltpu.VMEM((2 * mine.shape[0], B), jnp.float32),
            pltpu.VMEM((n, x.shape[0], B), jnp.float32),
        ],
        compiler_params=pltpu.CompilerParams(vmem_limit_bytes=12 << 20),
        cost_estimate=pl.CostEstimate(flops=20_000_000_000, bytes_accessed=4_000_000, transcendentals=0),
        name="whiten",
    )(bit, mine, other, x)


def gram_kernel(n, bit_ref, x_ref, keep_ref, send_ref, all_ref):
    turned = x_ref[...].T
    for j in range(n):
        all_ref[first(j, n) : first(j + 1, n)] = jnp.dot(
            turned[j * B :], x_ref[:, j * B : j * B + B], precision=HI, preferred_element_type=jnp.float32
        )
    half = keep_ref.shape[0]
    bit = bit_ref[0]
    keep_ref[...] = all_ref[pl.ds(pl.multiple_of(bit * half, 8), half)]
    send_ref[...] = all_ref[pl.ds(pl.multiple_of((1 - bit) * half, 8), half)]


def gram_halves(bit, x):
    n = x.shape[1] // B
    rows = first(n, n)
    return pl.pallas_call(
        functools.partial(gram_kernel, n),
        out_shape=[jax.ShapeDtypeStruct((rows // 2, B), jnp.float32)] * 2,
        in_specs=[SCALAR, VMEM],
        out_specs=[VMEM, VMEM],
        scratch_shapes=[pltpu.VMEM((rows, B), jnp.float32)],
        compiler_params=pltpu.CompilerParams(vmem_limit_bytes=12 << 20),
        cost_estimate=pl.CostEstimate(flops=700_000_000, bytes_accessed=2_000_000, transcendentals=0),
        name="gram",
    )(bit, x)


def cut_kernel(terms, order, at_ref, *refs):
    ins, outs, total_ref = refs[:terms], refs[terms:-1], refs[-1]
    total_ref[...] = functools.reduce(lambda a, b: a + b, [r[...] for r in ins])
    size = outs[0].shape[0]
    for s, out in enumerate(outs):
        out[...] = total_ref[pl.ds(pl.multiple_of(order(at_ref[0], s) * size, 8), size)]


def cut(at, arrays, pieces, rows, name):
    return pl.pallas_call(
        functools.partial(cut_kernel, len(arrays), lambda a, s: (a + s) & (pieces - 1)),
        out_shape=[jax.ShapeDtypeStruct((rows // pieces, B), jnp.float32)] * pieces,
        in_specs=[SCALAR] + [VMEM] * len(arrays),
        out_specs=[VMEM] * pieces,
        scratch_shapes=[pltpu.VMEM((rows, B), jnp.float32)],
        compiler_params=pltpu.CompilerParams(vmem_limit_bytes=6 << 20),
        cost_estimate=pl.CostEstimate(flops=1_000_000, bytes_accessed=3_000_000, transcendentals=0),
        name=name,
    )(at, *arrays)


def place_kernel(at_ref, *refs):
    out = refs[-1]
    count = len(refs) - 1
    size = refs[0].shape[0]
    for s in range(count):
        out[pl.ds(pl.multiple_of(((at_ref[0] - s) & (count - 1)) * size, 8), size)] = refs[s][...]


def place(at, arrays, name):
    rows = arrays[0].shape[0] * len(arrays)
    return pl.pallas_call(
        place_kernel,
        out_shape=jax.ShapeDtypeStruct((rows, B), jnp.float32),
        in_specs=[SCALAR] + [VMEM] * len(arrays),
        out_specs=VMEM,
        compiler_params=pltpu.CompilerParams(vmem_limit_bytes=6 << 20),
        cost_estimate=pl.CostEstimate(flops=0, bytes_accessed=1_500_000, transcendentals=0),
        name=name,
    )(at, *arrays)


def shifted(value, axis, by):
    size = lax.axis_size(axis)
    return lax.ppermute(value, axis, [(i, (i + by) % size) for i in range(size)])


def swapped(value, axis, by):
    return lax.ppermute(value, axis, [(i, i ^ by) for i in range(lax.axis_size(axis))])


def index(axis):
    return lax.axis_index(axis).reshape(1)


def reduced(pieces, axis):
    return jnp.sum(lax.all_to_all(pieces, axis, 0, 0, tiled=True), axis=0)


def spread(value, axis):
    copies = jnp.broadcast_to(value[None], (lax.axis_size(axis), *value.shape))
    return lax.all_to_all(copies, axis, 0, 0, tiled=True)


def x_pieces(keep, send):
    return cut(index("x"), [keep, swapped(send, "core", 1)], 4, keep.shape[0], "cut_x")


def x_sum(pieces):
    return functools.reduce(lambda a, b: a + b, [pieces[0]] + [shifted(pieces[s], "x", s) for s in (1, 2, 3)])


def gram_sum(mine):
    rows = mine.shape[0]
    mine = reduced(mine.reshape(8, rows // 8, B), "y")
    mine = jnp.sum(spread(mine, "z"), axis=0)
    mine = spread(mine, "y").reshape(rows, B)
    mine = place(index("x"), [mine] + [shifted(mine, "x", s) for s in (1, 2, 3)], "place_x")
    return mine, swapped(mine, "core", 1)


def body(embeddings, assignments):
    rows_here, width = embeddings.shape
    rows_axes = ("z", "y", "core")
    owners = lax.axis_size(rows_axes)
    total = rows_here * owners * lax.axis_size("x")
    per_owner = CENTROIDS // owners
    n = width // B
    bit = index("core")
    pieces = x_pieces(*gram_halves(bit, embeddings))

    target = assignments // per_owner
    local = assignments % per_owner
    same = target[:, None] == target[None, :]
    before = jnp.arange(rows_here)[:, None] > jnp.arange(rows_here)[None, :]
    rank = jnp.sum((same & before).astype(jnp.int32), axis=1)
    slot = target * CAP + rank
    chosen = slot[None, :] == jnp.arange(owners * CAP, dtype=jnp.int32)[:, None]
    outgoing = jnp.dot(
        chosen.astype(jnp.float32), embeddings, precision=lax.Precision.HIGHEST, preferred_element_type=jnp.float32
    )
    labels = jnp.sum(jnp.where(chosen, (local + 1)[None, :], 0), axis=1) - 1
    outgoing = outgoing.reshape(owners, CAP * width)
    labels = jnp.pad(labels.reshape(owners, CAP).astype(jnp.float32), ((0, 0), (0, B - CAP)))
    packed = jnp.concatenate([outgoing, labels], axis=1).reshape(owners, 1, CAP * width + B)
    packed = lax.all_to_all(packed, rows_axes, 0, 0, tiled=True)
    summed, packed = lax.optimization_barrier((x_sum(pieces), packed))
    packed = packed.reshape(owners, CAP * width + B)
    incoming = packed[:, : CAP * width].reshape(owners * CAP, width)
    tags = packed[:, CAP * width : CAP * width + CAP].reshape(-1).astype(jnp.int32)
    member = (tags[None, :] == jnp.arange(per_owner, dtype=jnp.int32)[:, None]).astype(jnp.float32)
    sums = jnp.dot(member, incoming, precision=lax.Precision.HIGHEST, preferred_element_type=jnp.float32)
    counts = jnp.sum(member, axis=1)
    groups = lax.axis_size("x")
    keep = per_owner // groups
    sums = sums.reshape(groups, keep * n, B)
    counts = jnp.pad(counts.reshape(groups, 1, keep), ((0, 0), (0, 7), (0, B - keep)))
    mine = reduced(jnp.concatenate([sums, counts], axis=1), "x")
    sums = mine[: keep * n].reshape(keep, width)
    counts = mine[keep * n, :keep]

    mine, other = gram_sum(summed)
    means = sums / jnp.maximum(counts, 1.0)[:, None]
    solved = whiten(bit, mine, other, jnp.concatenate([embeddings, means], axis=0), total)
    return solved[:rows_here], solved[rows_here:]


def solution(mesh):
    fine = Mesh(mesh.devices.reshape(8, 8, 2, 4), ("z", "y", "core", "x"))
    spec = ("z", "y", "core", "x")
    return jax.shard_map(
        body,
        mesh=fine,
        in_specs=(P(spec, None), P(spec)),
        out_specs=(P(spec, None), P(spec, None)),
        check_vma=False,
    )
```

```python
import functools

import jax
import jax.numpy as jnp
from jax import lax
from jax.experimental import pallas as pl
from jax.experimental.pallas import tpu as pltpu
from jax.sharding import Mesh, PartitionSpec as P

CENTROIDS = 16384
CAP = 2
B = 128

VMEM = pl.BlockSpec(memory_space=pltpu.VMEM)
SCALAR = pl.BlockSpec(memory_space=pltpu.SMEM)
HI = lax.Precision.HIGHEST
NT = (((1,), (1,)), ((), ()))


def mul_t(a, b):
    return lax.dot_general(a, b, NT, precision=HI, preferred_element_type=jnp.float32)


def inverse_factor(block):
    groups = B // 8
    tiles = [block[8 * i : 8 * i + 8] for i in range(groups)]
    lane = lax.broadcasted_iota(jnp.int32, (8, B), 1)
    sub = lax.broadcasted_iota(jnp.int32, (8, B), 0)
    for g in range(groups):
        done = (lane >= 8 * g) & (lane < 8 * g + 8)

        def columns(tile):
            return [jnp.broadcast_to(tile[:, 8 * g + k : 8 * g + k + 1], (8, B)) for k in range(8)]

        own = columns(tiles[g])
        s = [[own[p][k : k + 1] for p in range(k + 1)] for k in range(8)]
        mult, recip = {}, []
        for p in range(0, 8, 2):
            a, e, c = s[p][p], s[p + 1][p], s[p + 1][p + 1]
            det = a * c - e * e
            r0, rd = 1.0 / a, 1.0 / det
            r1, both = a * rd, r0 * rd
            mult[p + 1, p] = m = e * r0
            second = {q: s[q][p + 1] - m * s[q][p] for q in range(p + 2, 8)}
            cross = {q: a * s[q][p + 1] - e * s[q][p] for q in range(p + 2, min(p + 4, 8))}
            for k in range(p + 2, 8):
                mult[k, p], mult[k, p + 1] = m0, m1 = s[k][p] * r0, second[k] * r1
                for q in range(k, 8):
                    if q in cross:
                        s[q][k] = (s[q][k] - (s[k][p] * s[q][p]) * r0) - (cross[k] * cross[q]) * both
                    else:
                        s[q][k] = (s[q][k] - m0 * s[q][p]) - m1 * second[q]
            s[p + 1][p + 1] = det * r0
            recip += [r0, r1]
        here = jnp.where(lane == sub + 8 * g, 1.0, jnp.where(done, 0.0, tiles[g]))
        rows = [jnp.broadcast_to(here[k : k + 1], (8, B)) for k in range(8)]
        for p in range(8):
            for k in range(p + 1, 8):
                rows[k] = rows[k] - mult[k, p] * rows[p]
        scaled = [rows[p] * recip[p] for p in range(8)]
        for i in range(g + 1, groups):
            new = jnp.where(done, 0.0, tiles[i])
            below = columns(tiles[i])
            for p in range(8):
                for k in range(p + 1, 8):
                    below[k] = below[k] - mult[k, p] * below[p]
                new = new - below[p] * scaled[p]
            tiles[i] = new
        final = rows[0] * lax.rsqrt(s[0][0])
        for k in range(1, 8):
            final = jnp.where(sub == k, rows[k] * lax.rsqrt(s[k][k]), final)
        tiles[g] = final
    row = lax.broadcasted_iota(jnp.int32, (B, B), 0)
    col = lax.broadcasted_iota(jnp.int32, (B, B), 1)
    return jnp.where(col <= row, jnp.concatenate(tiles, axis=0), 0.0)


def first(j, n):
    return (j * n - j * (j - 1) // 2) * B


def block(i, j, n, base=0):
    at = first(j, n) - first(base, n) + (i - j) * B
    return slice(at, at + B)


def steps(which, n, inv, load, store, x_blocks, panel_ref, inv_ref):
    base = which[0]
    for now in which:
        rest = range(now + 1, n)
        panel = {i: mul_t(load(now, i, now), inv) for i in rest}
        if rest:
            following = inverse_factor(load(now, now + 1, now + 1) - mul_t(panel[now + 1], panel[now + 1]))
        x_blocks[now] = solved = mul_t(x_blocks[now], inv)
        for j in rest:
            at = (j - now - 1) * B + sum(n - 1 - t for t in range(base, now)) * B
            panel_ref[at : at + B] = panel[j]
            for i in range(j, n):
                if i > now + 1:
                    store(now, i, j, load(now, i, j) - mul_t(panel[i], panel[j]))
            x_blocks[j] -= mul_t(solved, panel[j])
        if rest:
            inv_ref[now + 1 - base] = inv = following


def early_kernel(total, n, cut_at, bit_ref, mine_ref, other_ref, x_ref, panel_ref, inv_ref, left_ref, x_blocks, a_ref):
    row = lax.broadcasted_iota(jnp.int32, (B, B), 0)
    col = lax.broadcasted_iota(jnp.int32, (B, B), 1)
    half = mine_ref.shape[0]
    bit = bit_ref[0]
    a_ref[pl.ds(pl.multiple_of(bit * half, 8), half)] = mine_ref[...] * (1.0 / total)
    a_ref[pl.ds(pl.multiple_of((1 - bit) * half, 8), half)] = other_ref[...] * (1.0 / total)
    for j in range(n):
        a_ref[block(j, j, n)] += jnp.where(row == col, 1e-05, 0.0)
        x_blocks[j] = x_ref[:, j * B : j * B + B]

    def load(now, i, j):
        return a_ref[block(i, j, n)]

    def store(now, i, j, value):
        if now + 1 < cut_at:
            a_ref[block(i, j, n)] = value
        else:
            left_ref[block(i, j, n, cut_at)] = value

    inv_ref[0] = inv = inverse_factor(load(0, 0, 0))
    steps(range(cut_at), n, inv, load, store, x_blocks, panel_ref, inv_ref)


def late_kernel(n, cut_at, inv_in, left_ref, x_in, out_ref, panel_ref, inv_ref, a_ref, x_blocks):
    x_blocks[...] = x_in[...]

    def load(now, i, j):
        return (left_ref if now == cut_at else a_ref)[block(i, j, n, cut_at)]

    def store(now, i, j, value):
        a_ref[block(i, j, n, cut_at)] = value

    inv_ref[0] = inv = inv_in[cut_at]
    steps(range(cut_at, n), n, inv, load, store, x_blocks, panel_ref, inv_ref)
    for j in range(n):
        out_ref[:, j * B : j * B + B] = x_blocks[j]


def means_kernel(n, cut_at, got_ref, early_panel, early_inv, late_panel, late_inv, out_ref):
    peers = got_ref.shape[0]
    keep = out_ref.shape[0]

    def gathered(j):
        return functools.reduce(lambda a, b: a + b, [got_ref[q, j * keep : j * keep + keep] for q in range(peers)])

    counts = jnp.maximum(gathered(n), 1.0)
    x = [gathered(j) / counts for j in range(n)]
    at = [0, 0]
    for now in range(n):
        late = int(now >= cut_at)
        inv = late_inv[now - cut_at] if late else early_inv[now]
        x[now] = mul_t(x[now], inv)
        out_ref[:, now * B : now * B + B] = x[now]
        for j in range(now + 1, n):
            panel = (early_panel, late_panel)[late][at[late] : at[late] + B]
            at[late] += B
            x[j] = x[j] - mul_t(x[now], panel)


def f32(*shape):
    return jax.ShapeDtypeStruct(shape, jnp.float32)


def local_call(kernel, outs, ins, name, scratch=(), limit=12, flops=10_000_000_000, scalars=0):
    return pl.pallas_call(
        kernel,
        out_shape=outs,
        in_specs=[SCALAR] * scalars + [VMEM] * (len(ins) - scalars),
        out_specs=[VMEM] * len(outs),
        scratch_shapes=[pltpu.VMEM(shape, jnp.float32) for shape in scratch],
        compiler_params=pltpu.CompilerParams(vmem_limit_bytes=limit << 20),
        cost_estimate=pl.CostEstimate(flops=flops, bytes_accessed=4_000_000, transcendentals=0),
        name=name,
    )(*ins)


def early(bit, mine, other, x, total, cut_at):
    n = x.shape[1] // B
    rows = first(n, n)
    panels = sum(n - 1 - t for t in range(cut_at)) * B
    outs = [f32(panels, B), f32(cut_at + 1, B, B), f32(rows - first(cut_at, n), B), f32(n, x.shape[0], B)]
    kernel = functools.partial(early_kernel, total, n, cut_at)
    return local_call(kernel, outs, [bit, mine, other, x], "early", [(rows, B)], scalars=1)


def late(inv, left, x_blocks, cut_at):
    n, rows, _ = x_blocks.shape
    panels = sum(n - 1 - t for t in range(cut_at, n)) * B
    outs = [f32(rows, n * B), f32(panels, B), f32(n - cut_at, B, B)]
    kernel = functools.partial(late_kernel, n, cut_at)
    return local_call(kernel, outs, [inv, left, x_blocks], "late", [left.shape, x_blocks.shape])


def sums_kernel(cap, n, groups, packed_ref, out_ref):
    rows = packed_ref.shape[0]
    per_owner = B
    keep = per_owner // groups
    width = n * B
    ids = lax.broadcasted_iota(jnp.int32, (rows, per_owner), 1).astype(jnp.float32)
    tn = (((0,), (0,)), ((), ()))
    members = []
    for c in range(cap):
        tag = packed_ref[:, cap * width + c : cap * width + c + 1]
        members.append(jnp.where(tag == ids, 1.0, 0.0))

    def summed(values):
        return functools.reduce(
            lambda a, b: a + b,
            [lax.dot_general(m, v, tn, precision=HI, preferred_element_type=jnp.float32) for m, v in zip(members, values)],
        )

    for j in range(n + 1):
        if j < n:
            part = summed([packed_ref[:, c * width + j * B : c * width + j * B + B] for c in range(cap)])
        else:
            part = summed([jnp.ones((rows, B), jnp.float32)] * cap)
        for q in range(groups):
            out_ref[q, j * keep : j * keep + keep] = part[q * keep : q * keep + keep]


def gram_kernel(n, bit_ref, x_ref, keep_ref, send_ref, all_ref):
    turned = x_ref[...].T
    for j in range(n):
        all_ref[first(j, n) : first(j + 1, n)] = jnp.dot(
            turned[j * B :], x_ref[:, j * B : j * B + B], precision=HI, preferred_element_type=jnp.float32
        )
    half = keep_ref.shape[0]
    bit = bit_ref[0]
    keep_ref[...] = all_ref[pl.ds(pl.multiple_of(bit * half, 8), half)]
    send_ref[...] = all_ref[pl.ds(pl.multiple_of((1 - bit) * half, 8), half)]


def gram_halves(bit, x):
    n = x.shape[1] // B
    rows = first(n, n)
    return pl.pallas_call(
        functools.partial(gram_kernel, n),
        out_shape=[jax.ShapeDtypeStruct((rows // 2, B), jnp.float32)] * 2,
        in_specs=[SCALAR, VMEM],
        out_specs=[VMEM, VMEM],
        scratch_shapes=[pltpu.VMEM((rows, B), jnp.float32)],
        compiler_params=pltpu.CompilerParams(vmem_limit_bytes=12 << 20),
        cost_estimate=pl.CostEstimate(flops=700_000_000, bytes_accessed=2_000_000, transcendentals=0),
        name="gram",
    )(bit, x)


def cut_kernel(terms, order, at_ref, *refs):
    ins, outs, total_ref = refs[:terms], refs[terms:-1], refs[-1]
    total_ref[...] = functools.reduce(lambda a, b: a + b, [r[...] for r in ins])
    size = outs[0].shape[0]
    for s, out in enumerate(outs):
        out[...] = total_ref[pl.ds(pl.multiple_of(order(at_ref[0], s) * size, 8), size)]


def cut(at, arrays, pieces, rows, name):
    return pl.pallas_call(
        functools.partial(cut_kernel, len(arrays), lambda a, s: (a + s) & (pieces - 1)),
        out_shape=[jax.ShapeDtypeStruct((rows // pieces, B), jnp.float32)] * pieces,
        in_specs=[SCALAR] + [VMEM] * len(arrays),
        out_specs=[VMEM] * pieces,
        scratch_shapes=[pltpu.VMEM((rows, B), jnp.float32)],
        compiler_params=pltpu.CompilerParams(vmem_limit_bytes=6 << 20),
        cost_estimate=pl.CostEstimate(flops=1_000_000, bytes_accessed=3_000_000, transcendentals=0),
        name=name,
    )(at, *arrays)


def place_kernel(at_ref, *refs):
    out = refs[-1]
    count = len(refs) - 1
    size = refs[0].shape[0]
    for s in range(count):
        out[pl.ds(pl.multiple_of(((at_ref[0] - s) & (count - 1)) * size, 8), size)] = refs[s][...]


def place(at, arrays, name):
    rows = arrays[0].shape[0] * len(arrays)
    return pl.pallas_call(
        place_kernel,
        out_shape=jax.ShapeDtypeStruct((rows, B), jnp.float32),
        in_specs=[SCALAR] + [VMEM] * len(arrays),
        out_specs=VMEM,
        compiler_params=pltpu.CompilerParams(vmem_limit_bytes=6 << 20),
        cost_estimate=pl.CostEstimate(flops=0, bytes_accessed=1_500_000, transcendentals=0),
        name=name,
    )(at, *arrays)


def shifted(value, axis, by):
    size = lax.axis_size(axis)
    return lax.ppermute(value, axis, [(i, (i + by) % size) for i in range(size)])


def swapped(value, axis, by):
    return lax.ppermute(value, axis, [(i, i ^ by) for i in range(lax.axis_size(axis))])


def index(axis):
    return lax.axis_index(axis).reshape(1)


def reduced(pieces, axis):
    return jnp.sum(lax.all_to_all(pieces, axis, 0, 0, tiled=True), axis=0)


def spread(value, axis):
    copies = jnp.broadcast_to(value[None], (lax.axis_size(axis), *value.shape))
    return lax.all_to_all(copies, axis, 0, 0, tiled=True)


def x_pieces(keep, send):
    return cut(index("x"), [keep, swapped(send, "core", 1)], 4, keep.shape[0], "cut_x")


def x_sum(pieces):
    return functools.reduce(lambda a, b: a + b, [pieces[0]] + [shifted(pieces[s], "x", s) for s in (1, 2, 3)])


def gram_sum(mine, packed):
    rows = mine.shape[0]
    mine = reduced(mine.reshape(8, rows // 8, B), "y")
    mine = jnp.sum(spread(mine, "z"), axis=0)
    mine = spread(mine, "y").reshape(rows, B)
    parts = [mine] + [shifted(mine, "x", s) for s in (1, 2, 3)]
    *parts[:2], packed = lax.optimization_barrier((*parts[:2], packed))
    packed = lax.all_to_all(packed, ("z", "y", "core"), 0, 0, tiled=True)
    mine = place(index("x"), parts, "place_x")
    return mine, swapped(mine, "core", 1), packed


def body(embeddings, assignments):
    rows_here, width = embeddings.shape
    rows_axes = ("z", "y", "core")
    owners = lax.axis_size(rows_axes)
    total = rows_here * owners * lax.axis_size("x")
    per_owner = CENTROIDS // owners
    n = width // B
    bit = index("core")
    pieces = x_pieces(*gram_halves(bit, embeddings))

    target = assignments // per_owner
    local = assignments % per_owner
    same = target[:, None] == target[None, :]
    before = jnp.arange(rows_here)[:, None] > jnp.arange(rows_here)[None, :]
    rank = jnp.sum((same & before).astype(jnp.int32), axis=1)
    slot = target * CAP + rank
    chosen = slot[None, :] == jnp.arange(owners * CAP, dtype=jnp.int32)[:, None]
    outgoing = jnp.dot(
        chosen.astype(jnp.float32), embeddings, precision=lax.Precision.HIGHEST, preferred_element_type=jnp.float32
    )
    labels = jnp.sum(jnp.where(chosen, (local + 1)[None, :], 0), axis=1) - 1
    outgoing = outgoing.reshape(owners, CAP * width)
    labels = jnp.pad(labels.reshape(owners, CAP).astype(jnp.float32), ((0, 0), (0, B - CAP)))
    packed = jnp.concatenate([outgoing, labels], axis=1).reshape(owners, 1, CAP * width + B)
    summed, packed = lax.optimization_barrier((x_sum(pieces), packed))
    mine, other, packed = gram_sum(summed, packed)
    cut_at = 2
    early_panel, early_inv, left, x_blocks = early(bit, mine, other, embeddings, total, cut_at)
    packed, early_inv = lax.optimization_barrier((packed, early_inv))
    groups = lax.axis_size("x")
    keep = per_owner // groups
    packed = packed.reshape(owners, CAP * width + B)
    kernel = functools.partial(sums_kernel, CAP, n, groups)
    [sums] = local_call(kernel, [f32(groups, (n + 1) * keep, B)], [packed], "sums", flops=400_000_000)
    sums = lax.all_to_all(sums, "x", 0, 0, tiled=True)
    whitened, late_panel, late_inv = late(early_inv, left, x_blocks, cut_at)
    sums, late_inv = lax.optimization_barrier((sums, late_inv))
    kernel = functools.partial(means_kernel, n, cut_at)
    panels = [sums, early_panel, early_inv, late_panel, late_inv]
    [means] = local_call(kernel, [f32(keep, width)], panels, "means", flops=400_000_000)
    return whitened, means


def solution(mesh):
    fine = Mesh(mesh.devices.reshape(8, 8, 2, 4), ("z", "y", "core", "x"))
    spec = ("z", "y", "core", "x")
    return jax.shard_map(
        body,
        mesh=fine,
        in_specs=(P(spec, None), P(spec)),
        out_specs=(P(spec, None), P(spec, None)),
        check_vma=False,
    )
```

```python
import functools

import jax
import jax.numpy as jnp
from jax import lax
from jax.experimental import pallas as pl
from jax.experimental.pallas import tpu as pltpu
from jax.sharding import Mesh, PartitionSpec as P

CENTROIDS = 16384
CAP = 2
B = 128

VMEM = pl.BlockSpec(memory_space=pltpu.VMEM)
SCALAR = pl.BlockSpec(memory_space=pltpu.SMEM)
HI = lax.Precision.HIGHEST
NT = (((1,), (1,)), ((), ()))


def mul_t(a, b):
    return lax.dot_general(a, b, NT, precision=HI, preferred_element_type=jnp.float32)


def inverse_factor(block):
    groups = B // 8
    tiles = [block[8 * i : 8 * i + 8] for i in range(groups)]
    lane = lax.broadcasted_iota(jnp.int32, (8, B), 1)
    sub = lax.broadcasted_iota(jnp.int32, (8, B), 0)
    for g in range(groups):
        done = (lane >= 8 * g) & (lane < 8 * g + 8)

        def columns(tile):
            return [jnp.broadcast_to(tile[:, 8 * g + k : 8 * g + k + 1], (8, B)) for k in range(8)]

        own = columns(tiles[g])
        s = [[own[p][k : k + 1] for p in range(k + 1)] for k in range(8)]
        mult, recip = {}, []
        for p in range(0, 8, 2):
            a, e, c = s[p][p], s[p + 1][p], s[p + 1][p + 1]
            det = a * c - e * e
            r0, rd = 1.0 / a, 1.0 / det
            r1, both = a * rd, r0 * rd
            mult[p + 1, p] = m = e * r0
            second = {q: s[q][p + 1] - m * s[q][p] for q in range(p + 2, 8)}
            cross = {q: a * s[q][p + 1] - e * s[q][p] for q in range(p + 2, min(p + 4, 8))}
            for k in range(p + 2, 8):
                mult[k, p], mult[k, p + 1] = m0, m1 = s[k][p] * r0, second[k] * r1
                for q in range(k, 8):
                    if q in cross:
                        s[q][k] = (s[q][k] - (s[k][p] * s[q][p]) * r0) - (cross[k] * cross[q]) * both
                    else:
                        s[q][k] = (s[q][k] - m0 * s[q][p]) - m1 * second[q]
            s[p + 1][p + 1] = det * r0
            recip += [r0, r1]
        here = jnp.where(lane == sub + 8 * g, 1.0, jnp.where(done, 0.0, tiles[g]))
        rows = [jnp.broadcast_to(here[k : k + 1], (8, B)) for k in range(8)]
        for p in range(8):
            for k in range(p + 1, 8):
                rows[k] = rows[k] - mult[k, p] * rows[p]
        scaled = [rows[p] * recip[p] for p in range(8)]
        for i in range(g + 1, groups):
            new = jnp.where(done, 0.0, tiles[i])
            below = columns(tiles[i])
            for p in range(8):
                for k in range(p + 1, 8):
                    below[k] = below[k] - mult[k, p] * below[p]
                new = new - below[p] * scaled[p]
            tiles[i] = new
        final = rows[0] * lax.rsqrt(s[0][0])
        for k in range(1, 8):
            final = jnp.where(sub == k, rows[k] * lax.rsqrt(s[k][k]), final)
        tiles[g] = final
    row = lax.broadcasted_iota(jnp.int32, (B, B), 0)
    col = lax.broadcasted_iota(jnp.int32, (B, B), 1)
    return jnp.where(col <= row, jnp.concatenate(tiles, axis=0), 0.0)


def first(j, n):
    return (j * n - j * (j - 1) // 2) * B


def block(i, j, n, base=0):
    at = first(j, n) - first(base, n) + (i - j) * B
    return slice(at, at + B)


def steps(which, n, inv, load, store, x_blocks, panel_ref, inv_ref, link_ref):
    base = which[0]
    for now in which:
        rest = range(now + 1, n)
        panel = {i: mul_t(load(now, i, now), inv) for i in rest}
        if rest:
            following = inverse_factor(load(now, now + 1, now + 1) - mul_t(panel[now + 1], panel[now + 1]))
        x_blocks[now] = solved = mul_t(x_blocks[now], inv)
        for j in rest:
            at = (j - now - 1) * B + sum(n - 1 - t for t in range(base, now)) * B
            panel_ref[at : at + B] = panel[j]
            for i in range(j, n):
                if i > now + 1:
                    store(now, i, j, load(now, i, j) - mul_t(panel[i], panel[j]))
            x_blocks[j] -= mul_t(solved, panel[j])
        if rest:
            link_ref[now - base] = jnp.dot(panel[now + 1], inv, precision=HI, preferred_element_type=jnp.float32)
            inv_ref[now + 1 - base] = inv = following


def early_kernel(total, n, cut_at, bit_ref, mine_ref, other_ref, x_ref, panel_ref, inv_ref, link_ref, left_ref, x_blocks, a_ref):
    row = lax.broadcasted_iota(jnp.int32, (B, B), 0)
    col = lax.broadcasted_iota(jnp.int32, (B, B), 1)
    half = mine_ref.shape[0]
    bit = bit_ref[0]
    a_ref[pl.ds(pl.multiple_of(bit * half, 8), half)] = mine_ref[...] * (1.0 / total)
    a_ref[pl.ds(pl.multiple_of((1 - bit) * half, 8), half)] = other_ref[...] * (1.0 / total)
    for j in range(n):
        a_ref[block(j, j, n)] += jnp.where(row == col, 1e-05, 0.0)
        x_blocks[j] = x_ref[:, j * B : j * B + B]

    def load(now, i, j):
        return a_ref[block(i, j, n)]

    def store(now, i, j, value):
        if now + 1 < cut_at:
            a_ref[block(i, j, n)] = value
        else:
            left_ref[block(i, j, n, cut_at)] = value

    inv_ref[0] = inv = inverse_factor(load(0, 0, 0))
    steps(range(cut_at), n, inv, load, store, x_blocks, panel_ref, inv_ref, link_ref)


def late_kernel(n, cut_at, inv_in, left_ref, x_in, out_ref, panel_ref, inv_ref, link_ref, a_ref, x_blocks):
    x_blocks[...] = x_in[...]

    def load(now, i, j):
        return (left_ref if now == cut_at else a_ref)[block(i, j, n, cut_at)]

    def store(now, i, j, value):
        a_ref[block(i, j, n, cut_at)] = value

    inv_ref[0] = inv = inv_in[cut_at]
    steps(range(cut_at, n), n, inv, load, store, x_blocks, panel_ref, inv_ref, link_ref)
    for j in range(n):
        out_ref[:, j * B : j * B + B] = x_blocks[j]


def means_kernel(n, cut_at, got_ref, panel0, inv0, link0, panel1, inv1, link1, out_ref):
    peers = got_ref.shape[0]
    keep = out_ref.shape[0]

    def gathered(j):
        return functools.reduce(lambda a, b: a + b, [got_ref[q, j * keep : j * keep + keep] for q in range(peers)])

    counts = jnp.maximum(gathered(n), 1.0)
    x = [gathered(j) / counts for j in range(n)]
    panels = [panel0[k * B : k * B + B] for k in range(panel0.shape[0] // B)]
    panels += [panel1[k * B : k * B + B] for k in range(panel1.shape[0] // B)]
    panels = iter(panels)
    for now in range(n):
        solved = mul_t(x[now], inv1[now - cut_at] if now >= cut_at else inv0[now])
        out_ref[:, now * B : now * B + B] = solved
        for j in range(now + 1, n):
            panel = next(panels)
            if j == now + 1:
                x[j] = x[j] - mul_t(x[now], link1[now - cut_at] if now >= cut_at else link0[now])
            else:
                x[j] = x[j] - mul_t(solved, panel)


def f32(*shape):
    return jax.ShapeDtypeStruct(shape, jnp.float32)


def local_call(kernel, outs, ins, name, scratch=(), limit=12, flops=10_000_000_000, scalars=0):
    return pl.pallas_call(
        kernel,
        out_shape=outs,
        in_specs=[SCALAR] * scalars + [VMEM] * (len(ins) - scalars),
        out_specs=[VMEM] * len(outs),
        scratch_shapes=[pltpu.VMEM(shape, jnp.float32) for shape in scratch],
        compiler_params=pltpu.CompilerParams(vmem_limit_bytes=limit << 20),
        cost_estimate=pl.CostEstimate(flops=flops, bytes_accessed=4_000_000, transcendentals=0),
        name=name,
    )(*ins)


def early(bit, mine, other, x, total, cut_at):
    n = x.shape[1] // B
    rows = first(n, n)
    panels = sum(n - 1 - t for t in range(cut_at)) * B
    outs = [f32(panels, B), f32(cut_at + 1, B, B), f32(cut_at, B, B), f32(rows - first(cut_at, n), B), f32(n, x.shape[0], B)]
    kernel = functools.partial(early_kernel, total, n, cut_at)
    return local_call(kernel, outs, [bit, mine, other, x], "early", [(rows, B)], scalars=1)


def late(inv, left, x_blocks, cut_at):
    n, rows, _ = x_blocks.shape
    panels = sum(n - 1 - t for t in range(cut_at, n)) * B
    outs = [f32(rows, n * B), f32(panels, B), f32(n - cut_at, B, B), f32(n - 1 - cut_at, B, B)]
    kernel = functools.partial(late_kernel, n, cut_at)
    return local_call(kernel, outs, [inv, left, x_blocks], "late", [left.shape, x_blocks.shape])


def sums_kernel(cap, n, groups, packed_ref, out_ref):
    rows = packed_ref.shape[0]
    per_owner = B
    keep = per_owner // groups
    width = n * B
    ids = lax.broadcasted_iota(jnp.int32, (rows, per_owner), 1).astype(jnp.float32)
    tn = (((0,), (0,)), ((), ()))
    members = []
    for c in range(cap):
        tag = packed_ref[:, cap * width + c : cap * width + c + 1]
        members.append(jnp.where(tag == ids, 1.0, 0.0))

    def summed(values):
        return functools.reduce(
            lambda a, b: a + b,
            [lax.dot_general(m, v, tn, precision=HI, preferred_element_type=jnp.float32) for m, v in zip(members, values)],
        )

    for j in range(n + 1):
        if j < n:
            part = summed([packed_ref[:, c * width + j * B : c * width + j * B + B] for c in range(cap)])
        else:
            part = summed([jnp.ones((rows, B), jnp.float32)] * cap)
        for q in range(groups):
            out_ref[q, j * keep : j * keep + keep] = part[q * keep : q * keep + keep]


def gram_kernel(n, bit_ref, x_ref, keep_ref, send_ref, all_ref):
    turned = x_ref[...].T
    for j in range(n):
        all_ref[first(j, n) : first(j + 1, n)] = jnp.dot(
            turned[j * B :], x_ref[:, j * B : j * B + B], precision=HI, preferred_element_type=jnp.float32
        )
    half = keep_ref.shape[0]
    bit = bit_ref[0]
    keep_ref[...] = all_ref[pl.ds(pl.multiple_of(bit * half, 8), half)]
    send_ref[...] = all_ref[pl.ds(pl.multiple_of((1 - bit) * half, 8), half)]


def gram_halves(bit, x):
    n = x.shape[1] // B
    rows = first(n, n)
    return pl.pallas_call(
        functools.partial(gram_kernel, n),
        out_shape=[jax.ShapeDtypeStruct((rows // 2, B), jnp.float32)] * 2,
        in_specs=[SCALAR, VMEM],
        out_specs=[VMEM, VMEM],
        scratch_shapes=[pltpu.VMEM((rows, B), jnp.float32)],
        compiler_params=pltpu.CompilerParams(vmem_limit_bytes=12 << 20),
        cost_estimate=pl.CostEstimate(flops=700_000_000, bytes_accessed=2_000_000, transcendentals=0),
        name="gram",
    )(bit, x)


def cut_kernel(terms, order, at_ref, *refs):
    ins, outs, total_ref = refs[:terms], refs[terms:-1], refs[-1]
    total_ref[...] = functools.reduce(lambda a, b: a + b, [r[...] for r in ins])
    size = outs[0].shape[0]
    for s, out in enumerate(outs):
        out[...] = total_ref[pl.ds(pl.multiple_of(order(at_ref[0], s) * size, 8), size)]


def cut(at, arrays, pieces, rows, name):
    return pl.pallas_call(
        functools.partial(cut_kernel, len(arrays), lambda a, s: (a + s) & (pieces - 1)),
        out_shape=[jax.ShapeDtypeStruct((rows // pieces, B), jnp.float32)] * pieces,
        in_specs=[SCALAR] + [VMEM] * len(arrays),
        out_specs=[VMEM] * pieces,
        scratch_shapes=[pltpu.VMEM((rows, B), jnp.float32)],
        compiler_params=pltpu.CompilerParams(vmem_limit_bytes=6 << 20),
        cost_estimate=pl.CostEstimate(flops=1_000_000, bytes_accessed=3_000_000, transcendentals=0),
        name=name,
    )(at, *arrays)


def place_kernel(at_ref, *refs):
    out = refs[-1]
    count = len(refs) - 1
    size = refs[0].shape[0]
    for s in range(count):
        out[pl.ds(pl.multiple_of(((at_ref[0] - s) & (count - 1)) * size, 8), size)] = refs[s][...]


def place(at, arrays, name):
    rows = arrays[0].shape[0] * len(arrays)
    return pl.pallas_call(
        place_kernel,
        out_shape=jax.ShapeDtypeStruct((rows, B), jnp.float32),
        in_specs=[SCALAR] + [VMEM] * len(arrays),
        out_specs=VMEM,
        compiler_params=pltpu.CompilerParams(vmem_limit_bytes=6 << 20),
        cost_estimate=pl.CostEstimate(flops=0, bytes_accessed=1_500_000, transcendentals=0),
        name=name,
    )(at, *arrays)


def shifted(value, axis, by):
    size = lax.axis_size(axis)
    return lax.ppermute(value, axis, [(i, (i + by) % size) for i in range(size)])


def swapped(value, axis, by):
    return lax.ppermute(value, axis, [(i, i ^ by) for i in range(lax.axis_size(axis))])


def index(axis):
    return lax.axis_index(axis).reshape(1)


def reduced(pieces, axis):
    return jnp.sum(lax.all_to_all(pieces, axis, 0, 0, tiled=True), axis=0)


def spread(value, axis):
    copies = jnp.broadcast_to(value[None], (lax.axis_size(axis), *value.shape))
    return lax.all_to_all(copies, axis, 0, 0, tiled=True)


def x_pieces(keep, send):
    return cut(index("x"), [keep, swapped(send, "core", 1)], 4, keep.shape[0], "cut_x")


def x_sum(pieces):
    return functools.reduce(lambda a, b: a + b, [pieces[0]] + [shifted(pieces[s], "x", s) for s in (1, 2, 3)])


def gram_sum(mine, packed):
    rows = mine.shape[0]
    mine = reduced(mine.reshape(8, rows // 8, B), "y")
    mine = jnp.sum(spread(mine, "z"), axis=0)
    mine = spread(mine, "y").reshape(rows, B)
    parts = [mine] + [shifted(mine, "x", s) for s in (1, 2, 3)]
    *parts[:2], packed = lax.optimization_barrier((*parts[:2], packed))
    packed = lax.all_to_all(packed, ("z", "y", "core"), 0, 0, tiled=True)
    mine = place(index("x"), parts, "place_x")
    return mine, swapped(mine, "core", 1), packed


def body(embeddings, assignments):
    rows_here, width = embeddings.shape
    rows_axes = ("z", "y", "core")
    owners = lax.axis_size(rows_axes)
    total = rows_here * owners * lax.axis_size("x")
    per_owner = CENTROIDS // owners
    n = width // B
    bit = index("core")
    pieces = x_pieces(*gram_halves(bit, embeddings))

    target = assignments // per_owner
    local = assignments % per_owner
    same = target[:, None] == target[None, :]
    before = jnp.arange(rows_here)[:, None] > jnp.arange(rows_here)[None, :]
    rank = jnp.sum((same & before).astype(jnp.int32), axis=1)
    slot = target * CAP + rank
    chosen = slot[None, :] == jnp.arange(owners * CAP, dtype=jnp.int32)[:, None]
    outgoing = jnp.dot(
        chosen.astype(jnp.float32), embeddings, precision=lax.Precision.HIGHEST, preferred_element_type=jnp.float32
    )
    labels = jnp.sum(jnp.where(chosen, (local + 1)[None, :], 0), axis=1) - 1
    outgoing = outgoing.reshape(owners, CAP * width)
    labels = jnp.pad(labels.reshape(owners, CAP).astype(jnp.float32), ((0, 0), (0, B - CAP)))
    packed = jnp.concatenate([outgoing, labels], axis=1).reshape(owners, 1, CAP * width + B)
    summed, packed = lax.optimization_barrier((x_sum(pieces), packed))
    mine, other, packed = gram_sum(summed, packed)
    cut_at = 3
    early_panel, early_inv, early_link, left, x_blocks = early(bit, mine, other, embeddings, total, cut_at)
    packed, early_inv = lax.optimization_barrier((packed, early_inv))
    groups = lax.axis_size("x")
    keep = per_owner // groups
    packed = packed.reshape(owners, CAP * width + B)
    kernel = functools.partial(sums_kernel, CAP, n, groups)
    [sums] = local_call(kernel, [f32(groups, (n + 1) * keep, B)], [packed], "sums", flops=400_000_000)
    sums = lax.all_to_all(sums, "x", 0, 0, tiled=True)
    whitened, late_panel, late_inv, late_link = late(early_inv, left, x_blocks, cut_at)
    sums, late_inv = lax.optimization_barrier((sums, late_inv))
    kernel = functools.partial(means_kernel, n, cut_at)
    panels = [sums, early_panel, early_inv, early_link, late_panel, late_inv, late_link]
    [means] = local_call(kernel, [f32(keep, width)], panels, "means", flops=400_000_000)
    return whitened, means


def solution(mesh):
    fine = Mesh(mesh.devices.reshape(8, 8, 2, 4), ("z", "y", "core", "x"))
    spec = ("z", "y", "core", "x")
    return jax.shard_map(
        body,
        mesh=fine,
        in_specs=(P(spec, None), P(spec)),
        out_specs=(P(spec, None), P(spec, None)),
        check_vma=False,
    )
```

```python
import functools

import jax
import jax.numpy as jnp
from jax import lax
from jax.experimental import pallas as pl
from jax.experimental.pallas import tpu as pltpu
from jax.sharding import Mesh, PartitionSpec as P

CENTROIDS = 16384
CAP = 2
B = 128

VMEM = pl.BlockSpec(memory_space=pltpu.VMEM)
SCALAR = pl.BlockSpec(memory_space=pltpu.SMEM)
HI = lax.Precision.HIGHEST
NT = (((1,), (1,)), ((), ()))


def mul_t(a, b):
    return lax.dot_general(a, b, NT, precision=HI, preferred_element_type=jnp.float32)


def inverse_factor(block):
    groups = B // 8
    tiles = [block[8 * i : 8 * i + 8] for i in range(groups)]
    lane = lax.broadcasted_iota(jnp.int32, (8, B), 1)
    sub = lax.broadcasted_iota(jnp.int32, (8, B), 0)
    for g in range(groups):
        done = (lane >= 8 * g) & (lane < 8 * g + 8)

        def columns(tile):
            return [jnp.broadcast_to(tile[:, 8 * g + k : 8 * g + k + 1], (8, B)) for k in range(8)]

        own = columns(tiles[g])
        s = [[own[p][k : k + 1] for p in range(k + 1)] for k in range(8)]
        mult, recip = {}, []
        for p in range(0, 8, 2):
            a, e, c = s[p][p], s[p + 1][p], s[p + 1][p + 1]
            det = a * c - e * e
            r0, rd = 1.0 / a, 1.0 / det
            r1, both = a * rd, r0 * rd
            mult[p + 1, p] = m = e * r0
            second = {q: s[q][p + 1] - m * s[q][p] for q in range(p + 2, 8)}
            cross = {q: a * s[q][p + 1] - e * s[q][p] for q in range(p + 2, min(p + 4, 8))}
            for k in range(p + 2, 8):
                mult[k, p], mult[k, p + 1] = m0, m1 = s[k][p] * r0, second[k] * r1
                for q in range(k, 8):
                    if q in cross:
                        s[q][k] = (s[q][k] - (s[k][p] * s[q][p]) * r0) - (cross[k] * cross[q]) * both
                    else:
                        s[q][k] = (s[q][k] - m0 * s[q][p]) - m1 * second[q]
            s[p + 1][p + 1] = det * r0
            recip += [r0, r1]
        here = jnp.where(lane == sub + 8 * g, 1.0, jnp.where(done, 0.0, tiles[g]))
        rows = [jnp.broadcast_to(here[k : k + 1], (8, B)) for k in range(8)]
        for p in range(8):
            for k in range(p + 1, 8):
                rows[k] = rows[k] - mult[k, p] * rows[p]
        scaled = [rows[p] * recip[p] for p in range(8)]
        for i in range(g + 1, groups):
            new = jnp.where(done, 0.0, tiles[i])
            below = columns(tiles[i])
            for p in range(8):
                for k in range(p + 1, 8):
                    below[k] = below[k] - mult[k, p] * below[p]
                new = new - below[p] * scaled[p]
            tiles[i] = new
        final = rows[0] * lax.rsqrt(s[0][0])
        for k in range(1, 8):
            final = jnp.where(sub == k, rows[k] * lax.rsqrt(s[k][k]), final)
        tiles[g] = final
    row = lax.broadcasted_iota(jnp.int32, (B, B), 0)
    col = lax.broadcasted_iota(jnp.int32, (B, B), 1)
    return jnp.where(col <= row, jnp.concatenate(tiles, axis=0), 0.0)


def first(j, n):
    return (j * n - j * (j - 1) // 2) * B


def block(i, j, n, base=0):
    at = first(j, n) - first(base, n) + (i - j) * B
    return slice(at, at + B)


def steps(which, n, inv, load, store, x_blocks, panel_ref, inv_ref, link_ref):
    base = which[0]
    for now in which:
        rest = range(now + 1, n)
        panel = {i: mul_t(load(now, i, now), inv) for i in rest}
        if rest:
            following = inverse_factor(load(now, now + 1, now + 1) - mul_t(panel[now + 1], panel[now + 1]))
        x_blocks[now] = solved = mul_t(x_blocks[now], inv)
        for j in rest:
            at = (j - now - 1) * B + sum(n - 1 - t for t in range(base, now)) * B
            panel_ref[at : at + B] = panel[j]
            for i in range(j, n):
                if i > now + 1:
                    store(now, i, j, load(now, i, j) - mul_t(panel[i], panel[j]))
            x_blocks[j] -= mul_t(solved, panel[j])
        if rest:
            link_ref[now - base] = jnp.dot(panel[now + 1], inv, precision=HI, preferred_element_type=jnp.float32)
            inv_ref[now + 1 - base] = inv = following


def early_kernel(total, n, cut_at, bit_ref, mine_ref, other_ref, x_ref, panel_ref, inv_ref, link_ref, left_ref, x_blocks, a_ref):
    row = lax.broadcasted_iota(jnp.int32, (B, B), 0)
    col = lax.broadcasted_iota(jnp.int32, (B, B), 1)
    half = mine_ref.shape[0]
    bit = bit_ref[0]
    a_ref[pl.ds(pl.multiple_of(bit * half, 8), half)] = mine_ref[...] * (1.0 / total)
    a_ref[pl.ds(pl.multiple_of((1 - bit) * half, 8), half)] = other_ref[...] * (1.0 / total)
    for j in range(n):
        a_ref[block(j, j, n)] += jnp.where(row == col, 1e-05, 0.0)
        x_blocks[j] = x_ref[:, j * B : j * B + B]

    def load(now, i, j):
        return a_ref[block(i, j, n)]

    def store(now, i, j, value):
        if now + 1 < cut_at:
            a_ref[block(i, j, n)] = value
        else:
            left_ref[block(i, j, n, cut_at)] = value

    inv_ref[0] = inv = inverse_factor(load(0, 0, 0))
    steps(range(cut_at), n, inv, load, store, x_blocks, panel_ref, inv_ref, link_ref)


def late_kernel(n, cut_at, inv_in, left_ref, x_in, out_ref, panel_ref, inv_ref, link_ref, a_ref, x_blocks):
    x_blocks[...] = x_in[...]

    def load(now, i, j):
        return (left_ref if now == cut_at else a_ref)[block(i, j, n, cut_at)]

    def store(now, i, j, value):
        a_ref[block(i, j, n, cut_at)] = value

    inv_ref[0] = inv = inv_in[cut_at]
    steps(range(cut_at, n), n, inv, load, store, x_blocks, panel_ref, inv_ref, link_ref)
    for j in range(n):
        out_ref[:, j * B : j * B + B] = x_blocks[j]


def means_kernel(n, cut_at, panel0, inv0, link0, panel1, inv1, link1, *refs):
    *got, out_ref = refs
    keep = out_ref.shape[0]

    def gathered(j):
        return functools.reduce(lambda a, b: a + b, [g[j * keep : j * keep + keep] for g in got])

    counts = jnp.maximum(gathered(n), 1.0)
    x = [gathered(j) / counts for j in range(n)]
    panels = [panel0[k * B : k * B + B] for k in range(panel0.shape[0] // B)]
    panels += [panel1[k * B : k * B + B] for k in range(panel1.shape[0] // B)]
    panels = iter(panels)
    for now in range(n):
        solved = mul_t(x[now], inv1[now - cut_at] if now >= cut_at else inv0[now])
        out_ref[:, now * B : now * B + B] = solved
        for j in range(now + 1, n):
            panel = next(panels)
            if j == now + 1:
                x[j] = x[j] - mul_t(x[now], link1[now - cut_at] if now >= cut_at else link0[now])
            else:
                x[j] = x[j] - mul_t(solved, panel)


def f32(*shape):
    return jax.ShapeDtypeStruct(shape, jnp.float32)


def local_call(kernel, outs, ins, name, scratch=(), limit=12, flops=10_000_000_000, scalars=0):
    return pl.pallas_call(
        kernel,
        out_shape=outs,
        in_specs=[SCALAR] * scalars + [VMEM] * (len(ins) - scalars),
        out_specs=[VMEM] * len(outs),
        scratch_shapes=[pltpu.VMEM(shape, jnp.float32) for shape in scratch],
        compiler_params=pltpu.CompilerParams(vmem_limit_bytes=limit << 20),
        cost_estimate=pl.CostEstimate(flops=flops, bytes_accessed=4_000_000, transcendentals=0),
        name=name,
    )(*ins)


def early(bit, mine, other, x, total, cut_at):
    n = x.shape[1] // B
    rows = first(n, n)
    panels = sum(n - 1 - t for t in range(cut_at)) * B
    outs = [f32(panels, B), f32(cut_at + 1, B, B), f32(cut_at, B, B), f32(rows - first(cut_at, n), B), f32(n, x.shape[0], B)]
    kernel = functools.partial(early_kernel, total, n, cut_at)
    return local_call(kernel, outs, [bit, mine, other, x], "early", [(rows, B)], scalars=1)


def late(inv, left, x_blocks, cut_at):
    n, rows, _ = x_blocks.shape
    panels = sum(n - 1 - t for t in range(cut_at, n)) * B
    outs = [f32(rows, n * B), f32(panels, B), f32(n - cut_at, B, B), f32(n - 1 - cut_at, B, B)]
    kernel = functools.partial(late_kernel, n, cut_at)
    return local_call(kernel, outs, [inv, left, x_blocks], "late", [left.shape, x_blocks.shape])


def sums_kernel(cap, n, at_ref, packed_ref, *refs):
    outs, all_ref = refs[:-1], refs[-1]
    rows = packed_ref.shape[0]
    groups = len(outs)
    keep = B // groups
    width = n * B
    ids = lax.broadcasted_iota(jnp.int32, (rows, B), 1).astype(jnp.float32)
    tn = (((0,), (0,)), ((), ()))
    tags = packed_ref[:, 0, cap * width : cap * width + B]
    members = [jnp.where(tags[:, c : c + 1] == ids, 1.0, 0.0) for c in range(cap)]

    def summed(values):
        return functools.reduce(
            lambda a, b: a + b,
            [lax.dot_general(m, v, tn, precision=HI, preferred_element_type=jnp.float32) for m, v in zip(members, values)],
        )

    for j in range(n + 1):
        if j < n:
            part = summed([packed_ref[:, 0, c * width + j * B : c * width + j * B + B] for c in range(cap)])
        else:
            part = summed([jnp.ones((rows, B), jnp.float32)] * cap)
        for q in range(groups):
            all_ref[q, j * keep : j * keep + keep] = part[q * keep : q * keep + keep]
    for s, out in enumerate(outs):
        out[...] = all_ref[(at_ref[0] + s) & (groups - 1)]


def gram_kernel(n, bit_ref, x_ref, keep_ref, send_ref, all_ref):
    turned = x_ref[...].T
    for j in range(n):
        all_ref[first(j, n) : first(j + 1, n)] = jnp.dot(
            turned[j * B :], x_ref[:, j * B : j * B + B], precision=HI, preferred_element_type=jnp.float32
        )
    half = keep_ref.shape[0]
    bit = bit_ref[0]
    keep_ref[...] = all_ref[pl.ds(pl.multiple_of(bit * half, 8), half)]
    send_ref[...] = all_ref[pl.ds(pl.multiple_of((1 - bit) * half, 8), half)]


def gram_halves(bit, x):
    n = x.shape[1] // B
    rows = first(n, n)
    return pl.pallas_call(
        functools.partial(gram_kernel, n),
        out_shape=[jax.ShapeDtypeStruct((rows // 2, B), jnp.float32)] * 2,
        in_specs=[SCALAR, VMEM],
        out_specs=[VMEM, VMEM],
        scratch_shapes=[pltpu.VMEM((rows, B), jnp.float32)],
        compiler_params=pltpu.CompilerParams(vmem_limit_bytes=12 << 20),
        cost_estimate=pl.CostEstimate(flops=700_000_000, bytes_accessed=2_000_000, transcendentals=0),
        name="gram",
    )(bit, x)


def cut_kernel(terms, order, at_ref, *refs):
    ins, outs, total_ref = refs[:terms], refs[terms:-1], refs[-1]
    total_ref[...] = functools.reduce(lambda a, b: a + b, [r[...] for r in ins])
    size = outs[0].shape[0]
    for s, out in enumerate(outs):
        out[...] = total_ref[pl.ds(pl.multiple_of(order(at_ref[0], s) * size, 8), size)]


def cut(at, arrays, pieces, rows, name):
    return pl.pallas_call(
        functools.partial(cut_kernel, len(arrays), lambda a, s: (a + s) & (pieces - 1)),
        out_shape=[jax.ShapeDtypeStruct((rows // pieces, B), jnp.float32)] * pieces,
        in_specs=[SCALAR] + [VMEM] * len(arrays),
        out_specs=[VMEM] * pieces,
        scratch_shapes=[pltpu.VMEM((rows, B), jnp.float32)],
        compiler_params=pltpu.CompilerParams(vmem_limit_bytes=6 << 20),
        cost_estimate=pl.CostEstimate(flops=1_000_000, bytes_accessed=3_000_000, transcendentals=0),
        name=name,
    )(at, *arrays)


def place_kernel(at_ref, *refs):
    out = refs[-1]
    count = len(refs) - 1
    size = refs[0].shape[0]
    for s in range(count):
        out[pl.ds(pl.multiple_of(((at_ref[0] - s) & (count - 1)) * size, 8), size)] = refs[s][...]


def place(at, arrays, name):
    rows = arrays[0].shape[0] * len(arrays)
    return pl.pallas_call(
        place_kernel,
        out_shape=jax.ShapeDtypeStruct((rows, B), jnp.float32),
        in_specs=[SCALAR] + [VMEM] * len(arrays),
        out_specs=VMEM,
        compiler_params=pltpu.CompilerParams(vmem_limit_bytes=6 << 20),
        cost_estimate=pl.CostEstimate(flops=0, bytes_accessed=1_500_000, transcendentals=0),
        name=name,
    )(at, *arrays)


def shifted(value, axis, by):
    size = lax.axis_size(axis)
    return lax.ppermute(value, axis, [(i, (i + by) % size) for i in range(size)])


def swapped(value, axis, by):
    return lax.ppermute(value, axis, [(i, i ^ by) for i in range(lax.axis_size(axis))])


def index(axis):
    return lax.axis_index(axis).reshape(1)


def reduced(pieces, axis):
    return jnp.sum(lax.all_to_all(pieces, axis, 0, 0, tiled=True), axis=0)


def spread(value, axis):
    copies = jnp.broadcast_to(value[None], (lax.axis_size(axis), *value.shape))
    return lax.all_to_all(copies, axis, 0, 0, tiled=True)


def x_pieces(keep, send):
    return cut(index("x"), [keep, swapped(send, "core", 1)], 4, keep.shape[0], "cut_x")


def x_sum(pieces):
    return functools.reduce(lambda a, b: a + b, [pieces[0]] + [shifted(pieces[s], "x", s) for s in (1, 2, 3)])


def gram_sum(mine, packed):
    rows = mine.shape[0]
    mine = reduced(mine.reshape(8, rows // 8, B), "y")
    mine = jnp.sum(spread(mine, "z"), axis=0)
    mine = spread(mine, "y").reshape(rows, B)
    parts = [mine] + [shifted(mine, "x", s) for s in (1, 2, 3)]
    *parts[:2], packed = lax.optimization_barrier((*parts[:2], packed))
    packed = lax.all_to_all(packed, ("z", "y", "core"), 0, 0, tiled=True)
    mine = place(index("x"), parts, "place_x")
    return mine, swapped(mine, "core", 1), packed


def body(embeddings, assignments):
    rows_here, width = embeddings.shape
    rows_axes = ("z", "y", "core")
    owners = lax.axis_size(rows_axes)
    total = rows_here * owners * lax.axis_size("x")
    per_owner = CENTROIDS // owners
    n = width // B
    bit = index("core")
    pieces = x_pieces(*gram_halves(bit, embeddings))

    target = assignments // per_owner
    local = assignments % per_owner
    same = target[:, None] == target[None, :]
    before = jnp.arange(rows_here)[:, None] > jnp.arange(rows_here)[None, :]
    rank = jnp.sum((same & before).astype(jnp.int32), axis=1)
    slot = target * CAP + rank
    chosen = slot[None, :] == jnp.arange(owners * CAP, dtype=jnp.int32)[:, None]
    outgoing = jnp.dot(
        chosen.astype(jnp.float32), embeddings, precision=lax.Precision.HIGHEST, preferred_element_type=jnp.float32
    )
    labels = jnp.sum(jnp.where(chosen, (local + 1)[None, :], 0), axis=1) - 1
    outgoing = outgoing.reshape(owners, CAP * width)
    labels = jnp.pad(labels.reshape(owners, CAP).astype(jnp.float32), ((0, 0), (0, B - CAP)))
    packed = jnp.concatenate([outgoing, labels], axis=1).reshape(owners, 1, CAP * width + B)
    summed, packed = lax.optimization_barrier((x_sum(pieces), packed))
    mine, other, packed = gram_sum(summed, packed)
    cut_at = 4
    early_panel, early_inv, early_link, left, x_blocks = early(bit, mine, other, embeddings, total, cut_at)
    packed, early_inv = lax.optimization_barrier((packed, early_inv))
    groups = lax.axis_size("x")
    keep = per_owner // groups
    kernel = functools.partial(sums_kernel, CAP, n)
    piece = ((n + 1) * keep, B)
    sums = local_call(
        kernel, [f32(*piece)] * groups, [index("x"), packed], "sums", [(groups, *piece)], flops=400_000_000, scalars=1
    )
    sums = [sums[0]] + [shifted(sums[s], "x", s) for s in range(1, groups)]
    whitened, *late_parts = late(early_inv, left, x_blocks, cut_at)
    *sums, late_parts[1] = lax.optimization_barrier((*sums, late_parts[1]))
    kernel = functools.partial(means_kernel, n, cut_at)
    parts = [early_panel, early_inv, early_link, *late_parts, *sums]
    [means] = local_call(kernel, [f32(keep, width)], parts, "means", flops=400_000_000)
    return whitened, means


def solution(mesh):
    fine = Mesh(mesh.devices.reshape(8, 8, 2, 4), ("z", "y", "core", "x"))
    spec = ("z", "y", "core", "x")
    return jax.shard_map(
        body,
        mesh=fine,
        in_specs=(P(spec, None), P(spec)),
        out_specs=(P(spec, None), P(spec, None)),
        check_vma=False,
    )
```

```python
import functools

import jax
import jax.numpy as jnp
from jax import lax
from jax.experimental import pallas as pl
from jax.experimental.pallas import tpu as pltpu
from jax.sharding import Mesh, PartitionSpec as P

CENTROIDS = 16384
CAP = 2
B = 128

VMEM = pl.BlockSpec(memory_space=pltpu.VMEM)
SCALAR = pl.BlockSpec(memory_space=pltpu.SMEM)
HI = lax.Precision.HIGHEST
NT = (((1,), (1,)), ((), ()))


def mul_t(a, b):
    return lax.dot_general(a, b, NT, precision=HI, preferred_element_type=jnp.float32)


def inverse_factor(block):
    groups = B // 8
    tiles = [block[8 * i : 8 * i + 8] for i in range(groups)]
    lane = lax.broadcasted_iota(jnp.int32, (8, B), 1)
    sub = lax.broadcasted_iota(jnp.int32, (8, B), 0)
    for g in range(groups):
        done = (lane >= 8 * g) & (lane < 8 * g + 8)

        def columns(tile):
            return [jnp.broadcast_to(tile[:, 8 * g + k : 8 * g + k + 1], (8, B)) for k in range(8)]

        own = columns(tiles[g])
        s = [[own[p][k : k + 1] for p in range(k + 1)] for k in range(8)]
        mult, recip = {}, []
        for p in range(0, 8, 2):
            a, e, c = s[p][p], s[p + 1][p], s[p + 1][p + 1]
            det = a * c - e * e
            r0, rd = 1.0 / a, 1.0 / det
            r1, both = a * rd, r0 * rd
            mult[p + 1, p] = m = e * r0
            second = {q: s[q][p + 1] - m * s[q][p] for q in range(p + 2, 8)}
            cross = {q: a * s[q][p + 1] - e * s[q][p] for q in range(p + 2, min(p + 4, 8))}
            for k in range(p + 2, 8):
                mult[k, p], mult[k, p + 1] = m0, m1 = s[k][p] * r0, second[k] * r1
                for q in range(k, 8):
                    if q in cross:
                        s[q][k] = (s[q][k] - (s[k][p] * s[q][p]) * r0) - (cross[k] * cross[q]) * both
                    else:
                        s[q][k] = (s[q][k] - m0 * s[q][p]) - m1 * second[q]
            s[p + 1][p + 1] = det * r0
            recip += [r0, r1]
        here = jnp.where(lane == sub + 8 * g, 1.0, jnp.where(done, 0.0, tiles[g]))
        rows = [jnp.broadcast_to(here[k : k + 1], (8, B)) for k in range(8)]
        for p in range(8):
            for k in range(p + 1, 8):
                rows[k] = rows[k] - mult[k, p] * rows[p]
        scaled = [rows[p] * recip[p] for p in range(8)]
        for i in range(g + 1, groups):
            new = jnp.where(done, 0.0, tiles[i])
            below = columns(tiles[i])
            for p in range(8):
                for k in range(p + 1, 8):
                    below[k] = below[k] - mult[k, p] * below[p]
                new = new - below[p] * scaled[p]
            tiles[i] = new
        final = rows[0] * lax.rsqrt(s[0][0])
        for k in range(1, 8):
            final = jnp.where(sub == k, rows[k] * lax.rsqrt(s[k][k]), final)
        tiles[g] = final
    row = lax.broadcasted_iota(jnp.int32, (B, B), 0)
    col = lax.broadcasted_iota(jnp.int32, (B, B), 1)
    return jnp.where(col <= row, jnp.concatenate(tiles, axis=0), 0.0)


def first(j, n):
    return (j * n - j * (j - 1) // 2) * B


def block(i, j, n, base=0):
    at = first(j, n) - first(base, n) + (i - j) * B
    return slice(at, at + B)


def steps(which, n, inv, load, store, x_blocks, panel_ref, inv_ref, link_ref):
    base = which[0]
    for now in which:
        rest = range(now + 1, n)
        panel = {i: mul_t(load(now, i, now), inv) for i in rest}
        if rest:
            following = inverse_factor(load(now, now + 1, now + 1) - mul_t(panel[now + 1], panel[now + 1]))
        x_blocks[now] = solved = mul_t(x_blocks[now], inv)
        for j in rest:
            at = (j - now - 1) * B + sum(n - 1 - t for t in range(base, now)) * B
            panel_ref[at : at + B] = panel[j]
            for i in range(j, n):
                if i > now + 1:
                    store(now, i, j, load(now, i, j) - mul_t(panel[i], panel[j]))
            x_blocks[j] -= mul_t(solved, panel[j])
        if rest:
            link_ref[now - base] = jnp.dot(panel[now + 1], inv, precision=HI, preferred_element_type=jnp.float32)
            inv_ref[now + 1 - base] = inv = following


def early_kernel(total, n, cut_at, bit_ref, mine_ref, other_ref, x_ref, panel_ref, inv_ref, link_ref, left_ref, x_blocks, a_ref):
    row = lax.broadcasted_iota(jnp.int32, (B, B), 0)
    col = lax.broadcasted_iota(jnp.int32, (B, B), 1)
    half = mine_ref.shape[0]
    bit = bit_ref[0]
    a_ref[pl.ds(pl.multiple_of(bit * half, 8), half)] = mine_ref[...] * (1.0 / total)
    a_ref[pl.ds(pl.multiple_of((1 - bit) * half, 8), half)] = other_ref[...] * (1.0 / total)
    for j in range(n):
        a_ref[block(j, j, n)] += jnp.where(row == col, 1e-05, 0.0)
        x_blocks[j] = x_ref[:, j * B : j * B + B]

    def load(now, i, j):
        return a_ref[block(i, j, n)]

    def store(now, i, j, value):
        if now + 1 < cut_at:
            a_ref[block(i, j, n)] = value
        else:
            left_ref[block(i, j, n, cut_at)] = value

    inv_ref[0] = inv = inverse_factor(load(0, 0, 0))
    steps(range(cut_at), n, inv, load, store, x_blocks, panel_ref, inv_ref, link_ref)


def late_kernel(n, cut_at, inv_in, left_ref, x_in, out_ref, panel_ref, inv_ref, link_ref, a_ref, x_blocks):
    x_blocks[...] = x_in[...]

    def load(now, i, j):
        return (left_ref if now == cut_at else a_ref)[block(i, j, n, cut_at)]

    def store(now, i, j, value):
        a_ref[block(i, j, n, cut_at)] = value

    inv_ref[0] = inv = inv_in[cut_at]
    steps(range(cut_at, n), n, inv, load, store, x_blocks, panel_ref, inv_ref, link_ref)
    for j in range(n):
        out_ref[:, j * B : j * B + B] = x_blocks[j]


def means_kernel(n, cut_at, panel0, inv0, link0, panel1, inv1, link1, *refs):
    *got, out_ref = refs
    keep = out_ref.shape[0]

    def gathered(j):
        return functools.reduce(lambda a, b: a + b, [g[j * keep : j * keep + keep] for g in got])

    counts = jnp.maximum(gathered(n), 1.0)
    x = [gathered(j) / counts for j in range(n)]
    panels = [panel0[k * B : k * B + B] for k in range(panel0.shape[0] // B)]
    panels += [panel1[k * B : k * B + B] for k in range(panel1.shape[0] // B)]
    panels = iter(panels)
    for now in range(n):
        solved = mul_t(x[now], inv1[now - cut_at] if now >= cut_at else inv0[now])
        out_ref[:, now * B : now * B + B] = solved
        for j in range(now + 1, n):
            panel = next(panels)
            if j == now + 1:
                x[j] = x[j] - mul_t(x[now], link1[now - cut_at] if now >= cut_at else link0[now])
            else:
                x[j] = x[j] - mul_t(solved, panel)


def f32(*shape):
    return jax.ShapeDtypeStruct(shape, jnp.float32)


def local_call(kernel, outs, ins, name, scratch=(), limit=12, flops=10_000_000_000, scalars=0):
    return pl.pallas_call(
        kernel,
        out_shape=outs,
        in_specs=[SCALAR] * scalars + [VMEM] * (len(ins) - scalars),
        out_specs=[VMEM] * len(outs),
        scratch_shapes=[pltpu.VMEM(shape, jnp.float32) for shape in scratch],
        compiler_params=pltpu.CompilerParams(vmem_limit_bytes=limit << 20),
        cost_estimate=pl.CostEstimate(flops=flops, bytes_accessed=4_000_000, transcendentals=0),
        name=name,
    )(*ins)


def early(bit, mine, other, x, total, cut_at):
    n = x.shape[1] // B
    rows = first(n, n)
    panels = sum(n - 1 - t for t in range(cut_at)) * B
    outs = [f32(panels, B), f32(cut_at + 1, B, B), f32(cut_at, B, B), f32(rows - first(cut_at, n), B), f32(n, x.shape[0], B)]
    kernel = functools.partial(early_kernel, total, n, cut_at)
    return local_call(kernel, outs, [bit, mine, other, x], "early", [(rows, B)], scalars=1)


def late(inv, left, x_blocks, cut_at):
    n, rows, _ = x_blocks.shape
    panels = sum(n - 1 - t for t in range(cut_at, n)) * B
    outs = [f32(rows, n * B), f32(panels, B), f32(n - cut_at, B, B), f32(n - 1 - cut_at, B, B)]
    kernel = functools.partial(late_kernel, n, cut_at)
    return local_call(kernel, outs, [inv, left, x_blocks], "late", [left.shape, x_blocks.shape], flops=100_000_000)


def sums_kernel(cap, n, at_ref, packed_ref, *refs):
    outs, all_ref = refs[:-1], refs[-1]
    rows = packed_ref.shape[0]
    groups = len(outs)
    keep = B // groups
    width = n * B
    ids = lax.broadcasted_iota(jnp.int32, (rows, B), 1).astype(jnp.float32)
    tn = (((0,), (0,)), ((), ()))
    tags = packed_ref[:, 0, cap * width : cap * width + B]
    members = [jnp.where(tags[:, c : c + 1] == ids, 1.0, 0.0) for c in range(cap)]

    def summed(values):
        return functools.reduce(
            lambda a, b: a + b,
            [lax.dot_general(m, v, tn, precision=HI, preferred_element_type=jnp.float32) for m, v in zip(members, values)],
        )

    for j in range(n + 1):
        if j < n:
            part = summed([packed_ref[:, 0, c * width + j * B : c * width + j * B + B] for c in range(cap)])
        else:
            part = summed([jnp.ones((rows, B), jnp.float32)] * cap)
        for q in range(groups):
            all_ref[q, j * keep : j * keep + keep] = part[q * keep : q * keep + keep]
    for s, out in enumerate(outs):
        out[...] = all_ref[(at_ref[0] + s) & (groups - 1)]


def gram_kernel(n, bit_ref, x_ref, keep_ref, send_ref, all_ref):
    turned = x_ref[...].T
    for j in range(n):
        all_ref[first(j, n) : first(j + 1, n)] = jnp.dot(
            turned[j * B :], x_ref[:, j * B : j * B + B], precision=HI, preferred_element_type=jnp.float32
        )
    half = keep_ref.shape[0]
    bit = bit_ref[0]
    keep_ref[...] = all_ref[pl.ds(pl.multiple_of(bit * half, 8), half)]
    send_ref[...] = all_ref[pl.ds(pl.multiple_of((1 - bit) * half, 8), half)]


def gram_halves(bit, x):
    n = x.shape[1] // B
    rows = first(n, n)
    return pl.pallas_call(
        functools.partial(gram_kernel, n),
        out_shape=[jax.ShapeDtypeStruct((rows // 2, B), jnp.float32)] * 2,
        in_specs=[SCALAR, VMEM],
        out_specs=[VMEM, VMEM],
        scratch_shapes=[pltpu.VMEM((rows, B), jnp.float32)],
        compiler_params=pltpu.CompilerParams(vmem_limit_bytes=12 << 20),
        cost_estimate=pl.CostEstimate(flops=700_000_000, bytes_accessed=2_000_000, transcendentals=0),
        name="gram",
    )(bit, x)


def cut_kernel(terms, order, at_ref, *refs):
    ins, outs, total_ref = refs[:terms], refs[terms:-1], refs[-1]
    total_ref[...] = functools.reduce(lambda a, b: a + b, [r[...] for r in ins])
    size = outs[0].shape[0]
    for s, out in enumerate(outs):
        out[...] = total_ref[pl.ds(pl.multiple_of(order(at_ref[0], s) * size, 8), size)]


def cut(at, arrays, pieces, rows, name):
    return pl.pallas_call(
        functools.partial(cut_kernel, len(arrays), lambda a, s: (a + s) & (pieces - 1)),
        out_shape=[jax.ShapeDtypeStruct((rows // pieces, B), jnp.float32)] * pieces,
        in_specs=[SCALAR] + [VMEM] * len(arrays),
        out_specs=[VMEM] * pieces,
        scratch_shapes=[pltpu.VMEM((rows, B), jnp.float32)],
        compiler_params=pltpu.CompilerParams(vmem_limit_bytes=6 << 20),
        cost_estimate=pl.CostEstimate(flops=1_000_000, bytes_accessed=3_000_000, transcendentals=0),
        name=name,
    )(at, *arrays)


def place_kernel(at_ref, *refs):
    out = refs[-1]
    count = len(refs) - 1
    size = refs[0].shape[0]
    for s in range(count):
        out[pl.ds(pl.multiple_of(((at_ref[0] - s) & (count - 1)) * size, 8), size)] = refs[s][...]


def place(at, arrays, name):
    rows = arrays[0].shape[0] * len(arrays)
    return pl.pallas_call(
        place_kernel,
        out_shape=jax.ShapeDtypeStruct((rows, B), jnp.float32),
        in_specs=[SCALAR] + [VMEM] * len(arrays),
        out_specs=VMEM,
        compiler_params=pltpu.CompilerParams(vmem_limit_bytes=6 << 20),
        cost_estimate=pl.CostEstimate(flops=0, bytes_accessed=1_500_000, transcendentals=0),
        name=name,
    )(at, *arrays)


def shifted(value, axis, by):
    size = lax.axis_size(axis)
    return lax.ppermute(value, axis, [(i, (i + by) % size) for i in range(size)])


def swapped(value, axis, by):
    return lax.ppermute(value, axis, [(i, i ^ by) for i in range(lax.axis_size(axis))])


def index(axis):
    return lax.axis_index(axis).reshape(1)


def reduced(pieces, axis):
    return jnp.sum(lax.all_to_all(pieces, axis, 0, 0, tiled=True), axis=0)


def spread(value, axis):
    copies = jnp.broadcast_to(value[None], (lax.axis_size(axis), *value.shape))
    return lax.all_to_all(copies, axis, 0, 0, tiled=True)


def x_pieces(keep, send):
    return cut(index("x"), [keep, swapped(send, "core", 1)], 4, keep.shape[0], "cut_x")


def x_sum(pieces):
    return functools.reduce(lambda a, b: a + b, [pieces[0]] + [shifted(pieces[s], "x", s) for s in (1, 2, 3)])


def gram_sum(mine, packed):
    rows = mine.shape[0]
    mine = reduced(mine.reshape(8, rows // 8, B), "y")
    mine = jnp.sum(spread(mine, "z"), axis=0)
    mine = spread(mine, "y").reshape(rows, B)
    parts = [mine] + [shifted(mine, "x", s) for s in (1, 2, 3)]
    *parts[:2], packed = lax.optimization_barrier((*parts[:2], packed))
    packed = lax.all_to_all(packed, ("z", "y", "core"), 0, 0, tiled=True)
    mine = place(index("x"), parts, "place_x")
    return mine, swapped(mine, "core", 1), packed


def body(embeddings, assignments):
    rows_here, width = embeddings.shape
    rows_axes = ("z", "y", "core")
    owners = lax.axis_size(rows_axes)
    total = rows_here * owners * lax.axis_size("x")
    per_owner = CENTROIDS // owners
    n = width // B
    bit = index("core")
    pieces = x_pieces(*gram_halves(bit, embeddings))

    target = assignments // per_owner
    local = assignments % per_owner
    same = target[:, None] == target[None, :]
    before = jnp.arange(rows_here)[:, None] > jnp.arange(rows_here)[None, :]
    rank = jnp.sum((same & before).astype(jnp.int32), axis=1)
    slot = target * CAP + rank
    chosen = slot[None, :] == jnp.arange(owners * CAP, dtype=jnp.int32)[:, None]
    outgoing = jnp.dot(
        chosen.astype(jnp.float32), embeddings, precision=lax.Precision.HIGHEST, preferred_element_type=jnp.float32
    )
    labels = jnp.sum(jnp.where(chosen, (local + 1)[None, :], 0), axis=1) - 1
    outgoing = outgoing.reshape(owners, CAP * width)
    labels = jnp.pad(labels.reshape(owners, CAP).astype(jnp.float32), ((0, 0), (0, B - CAP)))
    packed = jnp.concatenate([outgoing, labels], axis=1).reshape(owners, 1, CAP * width + B)
    summed, packed = lax.optimization_barrier((x_sum(pieces), packed))
    mine, other, packed = gram_sum(summed, packed)
    cut_at = 4
    early_panel, early_inv, early_link, left, x_blocks = early(bit, mine, other, embeddings, total, cut_at)
    whitened, *late_parts = late(early_inv, left, x_blocks, cut_at)
    packed, late_parts[1] = lax.optimization_barrier((packed, late_parts[1]))
    groups = lax.axis_size("x")
    keep = per_owner // groups
    kernel = functools.partial(sums_kernel, CAP, n)
    piece = ((n + 1) * keep, B)
    sums = local_call(
        kernel, [f32(*piece)] * groups, [index("x"), packed], "sums", [(groups, *piece)], flops=400_000_000, scalars=1
    )
    sums = [sums[0]] + [shifted(sums[s], "x", s) for s in range(1, groups)]
    kernel = functools.partial(means_kernel, n, cut_at)
    parts = [early_panel, early_inv, early_link, *late_parts, *sums]
    [means] = local_call(kernel, [f32(keep, width)], parts, "means", flops=400_000_000)
    return whitened, means


def solution(mesh):
    fine = Mesh(mesh.devices.reshape(8, 8, 2, 4), ("z", "y", "core", "x"))
    spec = ("z", "y", "core", "x")
    return jax.shard_map(
        body,
        mesh=fine,
        in_specs=(P(spec, None), P(spec)),
        out_specs=(P(spec, None), P(spec, None)),
        check_vma=False,
    )
```
